256 devices in a mesh: seq: 32 (over y_hi, z, core), batch: 8 (over x, y_lo).
Axes of the slice: x: 4, y: 4 (y_hi: 2, y_lo: 2; y = y_hi * 2 + y_lo), z: 8, core: 2. Of those that a mesh axis runs over, the one named last changes fastest.
Arguments:
- tokens: int32 [32768], P(('batch', 'seq')), parts along dimension 0, may hold values from 0 to 4
- fwd_states: bfloat16 [32768, 1024], P(('batch', 'seq')), parts along dimension 0, may hold values from -6 to 6
- rev_states: bfloat16 [32768, 1024], P(('batch', 'seq')), parts along dimension 0, may hold values from -6 to 6
- conv_weight: float32 [4, 1024], replicated, may hold values from -3 to 3
- embedding: float32 [5, 1024], replicated, may hold values from -80 to 80
- in_weight: bfloat16 [1024, 3072], P(None, 'seq'), may hold values from -0.1875 to 0.1875
- pack_query: bfloat16 [256, 1024], replicated, may hold values from -2000 to 2000
- pack_gain: float32 [1024], replicated, may hold values from 0.3 to 3
- tail_weight: bfloat16 [1024, 3072], P(None, 'seq'), may hold values from -0.1875 to 0.1875
- channel_perm: int32 [1024], replicated, may hold values from 0 to 1023, each once
Outputs:
- conjoined: bfloat16 [32768, 1024], P(('batch', 'seq')), parts along dimension 0
The draws below stay inside these ranges and needn't reach their ends.
There are 8 independent parts, one for each index of `batch`. The reference program is written for one: setup_inputs(seed, part) draws one part's arguments, and reference() takes and returns one part's arrays. A program takes and returns all parts, laid end to end along the dimension named above; an argument that names none is the same for every part. Nothing has to cross between parts.
Inputs may be any that keep to these rules, and one draw needn't show every extreme that they name: `tokens`: base ids: 0 A, 1 C, 2 G, 3 T, 4 N. `channel_perm`: each channel index appears once.
All inputs are finite; a program needn't handle non-finite values.
Results may differ from the reference program's by a relative error of at most 0.039.
Values may be sent and summed in bfloat16 or wider, within the bound.
No kernel may reach another device: no remote copies, remote signals or barrier semaphores. Data moves between devices by JAX's collectives and lax.ppermute only.
A program may use at most 128 MiB of HBM per device.

```python
import math
import jax
import jax.numpy as jnp
from jax import lax

D = 1024
PACK = 256
DH = 64
KW = 4
NPOS = 4096


def draw_pack_query(key, part):
    key = jax.random.fold_in(key, 7)
    values = 4.0 * jnp.clip(jax.random.normal(key, (PACK, D), jnp.float32), -6.0, 6.0)
    return values.astype(jnp.bfloat16)


def draw_embedding(key, part):
    key = jax.random.fold_in(key, 9)
    values = jnp.clip(jax.random.normal(key, (5, D), jnp.float32), -6.0, 6.0)
    return values.astype(jnp.float32)


def touch_ends(drawn, key, low, high):
    index_at = [jax.random.randint(jax.random.fold_in(key, axis), (), 0, length) for axis, length in enumerate(drawn.shape)]
    main_axis = drawn.shape.index(max(drawn.shape))
    next_to = index_at[:main_axis] + [(index_at[main_axis] + 1) % drawn.shape[main_axis]] + index_at[main_axis + 1:]
    return drawn.at[tuple(index_at)].set(low).at[tuple(next_to)].set(high)


def level_of(own_key, shape, split, smallest, largest):
    gain = 1.0
    for position, shards_of in split:
        steps = jax.random.uniform(jax.random.fold_in(jax.random.fold_in(own_key, 6), position), (shards_of,), jnp.float32, smallest / len(split), largest / len(split))
        gain = gain * jnp.repeat(jnp.exp(steps), shape[position] // shards_of).reshape((-1,) + (1,) * (len(shape) - 1 - position))
    return gain


def noise(key, dims, width, limit, split=(), held_as=jnp.bfloat16):
    loudness = level_of(key, dims, split, -0.22, 0.18) if split else 1.0
    array = jax.random.normal(key, dims, jnp.float32) * width * loudness
    return jnp.minimum(jnp.maximum(array, -limit), limit).astype(held_as)


def setup_inputs(seed: int = 0, part: int = 0) -> dict:
    seeds = jax.random.split(jax.random.key(seed), 11)
    part_splits = jax.random.split(jax.random.fold_in(seeds[10], part), 11)
    tokens = touch_ends(jax.random.randint(part_splits[0], (NPOS,), 0, 5), jax.random.fold_in(part_splits[0], 1), 0, 4).astype(jnp.int32)
    fwd_states = noise(part_splits[1], (NPOS, D), 1.0, 6.0, ((0, 32),))
    rev_states = noise(part_splits[2], (NPOS, D), 1.0, 6.0, ((0, 32),))
    conv_weight = noise(seeds[3], (KW, D), 0.5, 3.0, (), jnp.float32)
    embedding = draw_embedding(jax.random.fold_in(seeds[10], 71), part)
    in_weight = noise(seeds[5], (D, 3 * D), D ** -0.5, 0.1875, ((1, 32),))
    pack_query = draw_pack_query(jax.random.fold_in(seeds[10], 71), part)
    pack_gain = jnp.clip(jnp.exp(jax.random.uniform(seeds[7], (D,), jnp.float32, math.log(0.3), math.log(3.0))), 0.3, 3.0)
    tail_weight = noise(seeds[8], (D, 3 * D), D ** -0.5, 0.1875, ((1, 32),))
    channel_perm = jax.random.permutation(seeds[9], D).astype(jnp.int32)
    return {"tokens": tokens, "fwd_states": fwd_states, "rev_states": rev_states, "conv_weight": conv_weight, "embedding": embedding, "in_weight": in_weight, "pack_query": pack_query, "pack_gain": pack_gain, "tail_weight": tail_weight, "channel_perm": channel_perm}


def complement(symbols):
    return jnp.where(symbols == 4, 4, 3 - symbols).astype(jnp.int32)

def embed(symbols, embedding):
    result = jnp.zeros((symbols.shape[0], embedding.shape[1]), jnp.float32)
    for symbol in range(5):
        result = result + jnp.where(symbols[:, None] == symbol, embedding[symbol][None, :], jnp.float32(0.0))
    return result

def shifted_sum(padded, conv_weight, length):
    kernel_taps = conv_weight.shape[0]
    total = jnp.zeros(padded.shape[:-2] + (length, padded.shape[-1]), jnp.float32)
    for lag_index in range(kernel_taps):
        begin = kernel_taps - 1 - lag_index
        total = total + conv_weight[lag_index] * padded[..., begin:begin + length, :]
    return total

def convolve(states, conv_weight):
    kernel_taps = conv_weight.shape[0]
    padded = jnp.pad(states.astype(jnp.float32), ((kernel_taps - 1, 0), (0, 0)))
    return shifted_sum(padded, conv_weight, states.shape[0])

def layer_norm(raw, pack_gain):
    centred = raw - lax.optimization_barrier(jnp.mean(raw, axis=-1, keepdims=True))
    spread = lax.optimization_barrier(jnp.mean(centred * centred, axis=-1, keepdims=True))
    return centred * lax.rsqrt(spread + 1e-06) * pack_gain

def reference(tokens, fwd_states, rev_states, conv_weight, embedding, in_weight, pack_query, pack_gain, tail_weight, channel_perm):
    half_rows = fwd_states.shape[0]
    heads = D // DH
    scale = 1.0 / math.sqrt(DH)
    fwd_hidden = convolve(fwd_states, conv_weight).astype(jnp.bfloat16)
    rev_hidden = convolve(rev_states, conv_weight).astype(jnp.bfloat16)
    rev_symbols = complement(tokens)[::-1]
    fwd_input = (fwd_hidden.astype(jnp.float32) + embed(tokens, embedding)).astype(jnp.bfloat16)
    rev_input = (rev_hidden.astype(jnp.float32) + embed(rev_symbols, embedding)).astype(jnp.bfloat16)
    inputs = jnp.concatenate([fwd_input, rev_input], axis=0)
    projected = jnp.dot(inputs, in_weight, preferred_element_type=jnp.float32).astype(jnp.bfloat16)
    pack_keys = projected[:, :D]
    pack_values = projected[:, D:2 * D]
    queries = projected[:, 2 * D:]

    def pack_head(head_index):
        offset = head_index * DH
        query_cols = lax.dynamic_slice_in_dim(pack_query, offset, DH, 1)
        key_cols = lax.dynamic_slice_in_dim(pack_keys, offset, DH, 1)
        value_cols = lax.dynamic_slice_in_dim(pack_values, offset, DH, 1)
        scores = jnp.dot(query_cols, key_cols.T, preferred_element_type=jnp.float32) * scale
        peak = lax.optimization_barrier(jnp.max(scores, axis=1, keepdims=True))
        expo = jnp.exp(scores - peak)
        total = lax.optimization_barrier(jnp.sum(expo, axis=1, keepdims=True))
        return jnp.dot(expo.astype(jnp.bfloat16), value_cols, preferred_element_type=jnp.float32) / total
    packed_heads = lax.map(pack_head, jnp.arange(heads, dtype=jnp.int32))
    raw = jnp.transpose(packed_heads, (1, 0, 2)).reshape(PACK, D)
    packed = layer_norm(raw, pack_gain).astype(jnp.bfloat16)
    unpack_kv = jnp.dot(packed, tail_weight[:, :2 * D], preferred_element_type=jnp.float32).astype(jnp.bfloat16)

    def unpack_head(head_index):
        offset = head_index * DH
        query_cols = lax.dynamic_slice_in_dim(queries, offset, DH, 1)
        key_cols = lax.dynamic_slice_in_dim(unpack_kv, offset, DH, 1)
        value_cols = lax.dynamic_slice_in_dim(unpack_kv, D + offset, DH, 1)
        scores = jnp.dot(query_cols, key_cols.T, preferred_element_type=jnp.float32) * scale
        weights = jax.nn.softmax(scores, axis=1).astype(jnp.bfloat16)
        return jnp.dot(weights, value_cols, preferred_element_type=jnp.float32).astype(jnp.bfloat16)
    attended_heads = lax.map(unpack_head, jnp.arange(heads, dtype=jnp.int32))
    attended = jnp.transpose(attended_heads, (1, 0, 2)).reshape(2 * half_rows, D)
    mixed = jnp.dot(attended, tail_weight[:, 2 * D:], preferred_element_type=jnp.float32)
    reverse_rows = mixed[half_rows:][::-1]
    return (mixed[:half_rows] + reverse_rows[:, channel_perm]).astype(jnp.bfloat16)
```

```python
import functools
import math

import jax
import jax.numpy as jnp
from jax import lax
from jax.experimental import pallas as pl
from jax.experimental.pallas import tpu as pltpu
from jax.sharding import PartitionSpec as P

DH = 64
STATS = 128
VMEM_LIMIT = 48 * 1024 * 1024
NT = (((1,), (1,)), ((), ()))
NN = (((1,), (0,)), ((), ()))

Z, X = 8, 4
AXES = ("seq", "batch")


def device_index(x, y, z, core):
    y_hi, y_lo = divmod(y % 4, 2)
    return (y_hi * 2 * Z + (z % Z) * 2 + core) * 2 * X + (x % X) * 2 + y_lo


def moves(target):
    return [
        (device_index(x, y, z, core), device_index(*target(x, y, z, core)))
        for x in range(X)
        for y in range(4)
        for z in range(Z)
        for core in range(2)
    ]


Z_UP = moves(lambda x, y, z, core: (x, y, z + 1, core))
Z_DOWN = moves(lambda x, y, z, core: (x, y, z - 1, core))
Y_OPPOSITE = moves(lambda x, y, z, core: (x, 3 - y, z, core))
CORE_SWAP = moves(lambda x, y, z, core: (x, y, z, 1 - core))


def send(shard, pairs):
    return lax.ppermute(shard, AXES, pairs)


def dot(a, b, dims):
    return lax.dot_general(a, b, dims, preferred_element_type=jnp.float32)


def complement(symbols):
    return jnp.where(symbols == 4, 4, 3 - symbols)


def embed(symbols, embedding):
    result = jnp.zeros((symbols.shape[0], embedding.shape[1]), jnp.float32)
    for symbol in range(5):
        result = result + jnp.where(
            symbols[:, None] == symbol, embedding[symbol][None, :], jnp.float32(0.0)
        )
    return result


def shifted_sum(padded, conv_weight, length):
    kernel_taps = conv_weight.shape[0]
    total = jnp.zeros(padded.shape[:-2] + (length, padded.shape[-1]), jnp.float32)
    for lag_index in range(kernel_taps):
        begin = kernel_taps - 1 - lag_index
        total = total + conv_weight[lag_index] * padded[..., begin : begin + length, :]
    return total


def strand_inputs(tokens, fwd_states, rev_states, conv_weight, embedding):
    local_len = tokens.shape[0]
    keep = local_len - conv_weight.shape[0] + 1
    count = lax.axis_size("seq")
    fwd_rim = lax.ppermute(fwd_states[keep:], "seq", [(i, i + 1) for i in range(count - 1)])
    rev_rim = lax.ppermute(
        rev_states[keep:], "seq", [(i, count - 2 - i) for i in range(count - 1)]
    )
    rev_here = lax.ppermute(rev_states, "seq", [(i, count - 1 - i) for i in range(count)])
    rims = jnp.stack([fwd_rim, rev_rim])
    stacked = jnp.stack([fwd_states, rev_here])
    extended = jnp.concatenate([rims, stacked], axis=1).astype(jnp.float32)
    hidden = shifted_sum(extended, conv_weight, local_len).astype(jnp.bfloat16)
    fwd_input = (hidden[0].astype(jnp.float32) + embed(tokens, embedding)).astype(jnp.bfloat16)
    rev_input = (
        hidden[1][::-1].astype(jnp.float32) + embed(complement(tokens), embedding)
    ).astype(jnp.bfloat16)
    return jnp.concatenate([fwd_input, rev_input], axis=0)


def ring_pieces(shard):
    columns = shard.shape[0]
    half = columns // 2
    first = jnp.stack([shard, send(shard, Y_OPPOSITE)])
    up, down = first, first
    pieces = [(0, 0, first)]
    for step in range(1, Z // 2):
        up, down = send(up, Z_UP), send(down, Z_DOWN)
        pieces += [(-step, 0, up), (step, 0, down)]
    pieces += [
        (-(Z // 2), 0, send(up[:, :half], Z_UP)),
        (Z // 2, half, send(down[:, half:], Z_DOWN)),
    ]
    return pieces


def pack_kernel(places, heads, x_own, x_other, query, seat, *refs):
    count = len(places)
    piece_refs = refs[:count]
    part_out, unpack_query_out = refs[count : count + 2]
    weight, inputs, sems = refs[count + 2 :]
    width = query.shape[1]
    half_width = width // 2
    y_hi, z, core = seat[0], seat[1], seat[2]
    columns = weight.shape[0] // 32
    copies = []
    for number, (step, begin, flip) in enumerate(places):
        source = piece_refs[number]
        rows = source.shape[1]
        where_z = lax.rem(z + step + Z, Z)
        where_core = 1 - core if flip else core
        for opposite in range(2):
            where_y = 1 - y_hi if opposite else y_hi
            place = (where_y * 2 * Z + where_z * 2 + where_core) * columns + begin
            place = pl.multiple_of(place, 16)
            copy = pltpu.make_async_copy(
                source.at[opposite], weight.at[pl.ds(place, rows)], sems.at[2 * number + opposite]
            )
            copy.start()
            copies.append(copy)
    own_rows = x_own.shape[0]
    inputs[:own_rows] = x_own[...]
    inputs[own_rows:] = x_other[...]
    for copy in copies:
        copy.wait()
    base = pl.multiple_of(core * half_width, half_width)
    rows_in = inputs[...]
    keys = dot(weight[pl.ds(base, half_width)], rows_in, NT).astype(jnp.bfloat16)
    values = dot(weight[pl.ds(base + width, half_width)], rows_in, NT).astype(jnp.bfloat16)
    unpack_query_out[...] = dot(x_own[...], weight[2 * width :], NT).astype(jnp.bfloat16)
    scale = 1.0 / math.sqrt(DH)
    slots = query.shape[0]
    lanes = lax.broadcasted_iota(jnp.int32, (slots, STATS), 1)
    peaks = jnp.zeros((slots, STATS), jnp.float32)
    totals = jnp.zeros((slots, STATS), jnp.float32)
    query_half = query[:, pl.ds(base, half_width)]
    held = None
    for head in range(heads // 2):
        cols = slice(head * DH, (head + 1) * DH)
        scores = dot(query_half[:, cols], keys[cols], NN) * scale
        peak = jnp.max(scores, axis=1, keepdims=True)
        expo = jnp.exp(scores - peak)
        peaks = jnp.where(lanes == head, peak, peaks)
        totals = jnp.where(lanes == head, jnp.sum(expo, axis=1, keepdims=True), totals)
        numer = dot(expo.astype(jnp.bfloat16), values[cols], NT)
        if head % 2:
            both = jnp.concatenate([held, numer], axis=1).astype(jnp.bfloat16)
            part_out[:, (head - 1) * DH : (head + 1) * DH] = both
        held = numer
    room = heads // 2
    stats = jnp.zeros((slots, STATS), jnp.float32)
    number = 0
    for value, terms in ((peaks, 3), (totals, 2)):
        for _ in range(terms):
            term = value.astype(jnp.bfloat16).astype(jnp.float32)
            value = value - term
            stats = stats + (pltpu.roll(term, number * room, 1) if number else term)
            number += 1
    part_out[:, half_width:] = stats.astype(jnp.bfloat16)


def merge_kernel(heads, parts, gain, packed_out):
    count, slots, _ = parts.shape
    half_width = packed_out.shape[1] // 2
    room = heads // 2
    stats = parts[:, :, half_width:].astype(jnp.float32).reshape(count * slots, STATS)

    def term(number):
        return pltpu.roll(stats, STATS - number * room, 1) if number else stats

    peaks = (term(0) + term(1) + term(2)).reshape(count // 2, 2, slots, STATS)
    totals = (term(3) + term(4)).reshape(count // 2, 2, slots, STATS)
    lanes = lax.broadcasted_iota(jnp.int32, peaks.shape, 3)
    peaks = jnp.where(lanes < room, peaks, 0.0)
    factors = jnp.exp(peaks - jnp.max(peaks, axis=0, keepdims=True))
    total = jnp.sum(factors * totals, axis=0)
    spread_rows = lax.broadcasted_iota(jnp.int32, (STATS, half_width), 0)
    spread_cols = lax.broadcasted_iota(jnp.int32, (STATS, half_width), 1)
    spread = ((spread_cols // DH) == spread_rows).astype(jnp.float32)

    def spread_out(value):
        return lax.dot_general(
            value, spread, NN, precision=lax.Precision.HIGHEST, preferred_element_type=jnp.float32
        )

    wide = spread_out(factors.reshape(count * slots, STATS)).reshape(
        count // 2, 2, slots, half_width
    )
    numer = parts[:, :, :half_width].astype(jnp.float32).reshape(wide.shape)
    numer = jnp.sum(wide * numer, axis=0)
    wide_total = spread_out(total.reshape(2 * slots, STATS)).reshape(2, slots, half_width)
    ratio = numer / wide_total
    raw = jnp.concatenate([ratio[0], ratio[1]], axis=1)
    centred = raw - jnp.mean(raw, axis=1, keepdims=True)
    variance = jnp.mean(centred * centred, axis=1, keepdims=True)
    packed_out[...] = (centred * lax.rsqrt(variance + 1e-06) * gain[...]).astype(jnp.bfloat16)


def tail_kernel(heads, packed_a, packed_b, queries, pairing, tail, out, weight, attended, sems):
    width = queries.shape[1]
    copies = []
    for number in range(3):
        rows = pl.ds(number * width, width)
        copy = pltpu.make_async_copy(tail.at[rows], weight.at[rows], sems.at[number])
        copy.start()
        copies.append(copy)
    packed = jnp.concatenate([packed_a[...], packed_b[...]], axis=0)
    copies[0].wait()
    keys = dot(weight[:width], packed, NT).astype(jnp.bfloat16)
    copies[1].wait()
    values = dot(packed, weight[width : 2 * width], NT).astype(jnp.bfloat16)
    scale = 1.0 / math.sqrt(DH)
    held = None
    for head in range(heads):
        cols = slice(head * DH, (head + 1) * DH)
        scores = dot(queries[:, cols], keys[cols], NN) * scale
        expo = jnp.exp(scores - jnp.max(scores, axis=1, keepdims=True))
        shares = (expo / jnp.sum(expo, axis=1, keepdims=True)).astype(jnp.bfloat16)
        result = dot(shares, values[:, cols], NN)
        if head % 2:
            both = jnp.concatenate([held, result], axis=1).astype(jnp.bfloat16)
            attended[:, (head - 1) * DH : (head + 1) * DH] = both
        held = result
    copies[2].wait()
    mixed = dot(attended[...], weight[2 * width :], NT)
    length = out.shape[0]
    reverse = mixed[length:]
    upper = reverse.astype(jnp.bfloat16)
    lower = (reverse - upper.astype(jnp.float32)).astype(jnp.bfloat16)
    paired = dot(upper, pairing[...], NN) + dot(lower, pairing[...], NN)
    out[...] = (mixed[:length] + paired).astype(jnp.bfloat16)


def params():
    return pltpu.CompilerParams(vmem_limit_bytes=VMEM_LIMIT)


VMEM = pl.BlockSpec(memory_space=pltpu.VMEM)
SMEM = pl.BlockSpec(memory_space=pltpu.SMEM)
ANY = pl.BlockSpec(memory_space=pl.ANY)


def shards(
    tokens,
    fwd_states,
    rev_states,
    conv_weight,
    embedding,
    in_weight,
    pack_query,
    pack_gain,
    tail_weight,
    channel_perm,
):
    local_len = tokens.shape[0]
    width = fwd_states.shape[1]
    slots = pack_query.shape[0]
    heads = width // DH
    count = lax.axis_size("seq")
    own_slots = slots // count
    place = lax.axis_index("seq")
    seat = jnp.stack([place // (2 * Z), place // 2 % Z, place % 2]).astype(jnp.int32)

    tail_cols = lax.all_gather(tail_weight.T, "seq", axis=0, tiled=True)
    own_pieces = ring_pieces(in_weight.T)
    x_own = strand_inputs(tokens, fwd_states, rev_states, conv_weight, embedding)
    x_other = send(x_own, CORE_SWAP)
    pairing = (
        lax.broadcasted_iota(jnp.int32, (width, width), 0) == channel_perm[None, :]
    ).astype(jnp.bfloat16)
    places, pieces = [], []
    for step, begin, piece in own_pieces:
        places += [(step, begin, False), (step, begin, True)]
        pieces += [piece, send(piece, CORE_SWAP)]

    part, queries = pl.pallas_call(
        functools.partial(pack_kernel, tuple(places), heads),
        out_shape=(
            jax.ShapeDtypeStruct((slots, width // 2 + STATS), jnp.bfloat16),
            jax.ShapeDtypeStruct((2 * local_len, width), jnp.bfloat16),
        ),
        in_specs=[VMEM, VMEM, VMEM, SMEM] + [ANY] * len(pieces),
        out_specs=(VMEM, VMEM),
        scratch_shapes=[
            pltpu.VMEM((3 * width, width), jnp.bfloat16),
            pltpu.VMEM((4 * local_len, width), jnp.bfloat16),
            pltpu.SemaphoreType.DMA((2 * len(pieces),)),
        ],
        compiler_params=params(),
        name="pack",
    )(x_own, x_other, pack_query, seat, *pieces)

    parts = lax.all_to_all(part.reshape(count, own_slots, -1), "seq", 0, 0)
    packed_own = pl.pallas_call(
        functools.partial(merge_kernel, heads),
        out_shape=jax.ShapeDtypeStruct((own_slots, width), jnp.bfloat16),
        in_specs=[VMEM, VMEM],
        out_specs=VMEM,
        compiler_params=params(),
        name="merge",
    )(parts, pack_gain[None, :])

    same_core = [list(range(core, count, 2)) for core in range(2)]
    copies = jnp.broadcast_to(packed_own[None], (count // 2, own_slots, width))
    packed_a = lax.all_to_all(copies, "seq", 0, 0, axis_index_groups=same_core)
    packed_a = packed_a.reshape(slots // 2, width)
    packed_b = send(packed_a, CORE_SWAP)

    return pl.pallas_call(
        functools.partial(tail_kernel, heads),
        out_shape=jax.ShapeDtypeStruct((local_len, width), jnp.bfloat16),
        in_specs=[VMEM, VMEM, VMEM, VMEM, ANY],
        out_specs=VMEM,
        scratch_shapes=[
            pltpu.VMEM((3 * width, width), jnp.bfloat16),
            pltpu.VMEM((2 * local_len, width), jnp.bfloat16),
            pltpu.SemaphoreType.DMA((3,)),
        ],
        compiler_params=params(),
        name="tail",
    )(packed_a, packed_b, queries, pairing, tail_cols)


def solution(mesh):
    in_specs = (
        P(("batch", "seq")),
        P(("batch", "seq"), None),
        P(("batch", "seq"), None),
        P(),
        P(),
        P(None, "seq"),
        P(),
        P(),
        P(None, "seq"),
        P(),
    )
    out_specs = P(("batch", "seq"), None)
    return jax.shard_map(shards, mesh=mesh, in_specs=in_specs, out_specs=out_specs, check_vma=False)
```

```python
import functools
import math

import jax
import jax.numpy as jnp
from jax import lax
from jax.experimental import pallas as pl
from jax.experimental.pallas import tpu as pltpu
from jax.sharding import PartitionSpec as P

DH = 64
STATS = 128
VMEM_LIMIT = 48 * 1024 * 1024
NT = (((1,), (1,)), ((), ()))
NN = (((1,), (0,)), ((), ()))

Z, X = 8, 4
AXES = ("seq", "batch")


def device_index(x, y, z, core):
    y_hi, y_lo = divmod(y % 4, 2)
    return (y_hi * 2 * Z + (z % Z) * 2 + core) * 2 * X + (x % X) * 2 + y_lo


def moves(target):
    return [
        (device_index(x, y, z, core), device_index(*target(x, y, z, core)))
        for x in range(X)
        for y in range(4)
        for z in range(Z)
        for core in range(2)
    ]


RING = moves(lambda x, y, z, core: (x, y, z + 1 - 2 * core, core))
Y_OPPOSITE = moves(lambda x, y, z, core: (x, 3 - y, z, core))
CORE_SWAP = moves(lambda x, y, z, core: (x, y, z, 1 - core))


def send(shard, pairs):
    return lax.ppermute(shard, AXES, pairs)


def dot(a, b, dims):
    return lax.dot_general(a, b, dims, preferred_element_type=jnp.float32)


def complement(symbols):
    return jnp.where(symbols == 4, 4, 3 - symbols)


def embed(symbols, embedding):
    result = jnp.zeros((symbols.shape[0], embedding.shape[1]), jnp.float32)
    for symbol in range(5):
        result = result + jnp.where(
            symbols[:, None] == symbol, embedding[symbol][None, :], jnp.float32(0.0)
        )
    return result


def shifted_sum(padded, conv_weight, length):
    kernel_taps = conv_weight.shape[0]
    total = jnp.zeros(padded.shape[:-2] + (length, padded.shape[-1]), jnp.float32)
    for lag_index in range(kernel_taps):
        begin = kernel_taps - 1 - lag_index
        total = total + conv_weight[lag_index] * padded[..., begin : begin + length, :]
    return total


def strand_inputs(tokens, fwd_states, rev_states, conv_weight, embedding):
    local_len = tokens.shape[0]
    keep = local_len - conv_weight.shape[0] + 1
    count = lax.axis_size("seq")
    fwd_rim = lax.ppermute(fwd_states[keep:], "seq", [(i, i + 1) for i in range(count - 1)])
    rev_rim = lax.ppermute(
        rev_states[keep:], "seq", [(i, count - 2 - i) for i in range(count - 1)]
    )
    rev_here = lax.ppermute(rev_states, "seq", [(i, count - 1 - i) for i in range(count)])
    rims = jnp.stack([fwd_rim, rev_rim])
    stacked = jnp.stack([fwd_states, rev_here])
    extended = jnp.concatenate([rims, stacked], axis=1).astype(jnp.float32)
    hidden = shifted_sum(extended, conv_weight, local_len).astype(jnp.bfloat16)
    fwd_input = (hidden[0].astype(jnp.float32) + embed(tokens, embedding)).astype(jnp.bfloat16)
    rev_input = (
        hidden[1][::-1].astype(jnp.float32) + embed(complement(tokens), embedding)
    ).astype(jnp.bfloat16)
    return jnp.concatenate([fwd_input, rev_input], axis=0)


def after(value, *others):
    return lax.optimization_barrier((value, *others))[0]


def ring_pieces(shard, core):
    half = shard.shape[0] // 2
    across = send(shard, Y_OPPOSITE)
    pieces = []
    held = [jnp.stack([mine, send(mine, CORE_SWAP)]) for mine in (shard, across)]
    for opposite in range(2):
        pieces.append(((opposite, 0, False, False), held[opposite]))
    for step in range(1, Z // 2 + 1):
        last = step == Z // 2
        for opposite in range(2):
            moved = held[opposite]
            if last:
                moved = lax.dynamic_slice_in_dim(moved, core * half, half, 1)
            moved = send(moved, RING)
            held[opposite] = moved
            pieces.append(((opposite, step, False, last), moved))
            pieces.append(((opposite, step, True, last), send(moved, CORE_SWAP)))
    return [place for place, _ in pieces], [piece for _, piece in pieces]


def start_copies(places, piece_refs, seat, weight, sems):
    y_hi, z, core = seat[0], seat[1], seat[2]
    columns = weight.shape[0] // 32
    copies = []
    for number, (opposite, step, swapped, halved) in enumerate(places):
        source = piece_refs[number]
        rows = source.shape[1]
        ring = 1 - core if swapped else core
        from_z = lax.rem(z + (2 * ring - 1) * step + Z, Z)
        from_y = 1 - y_hi if opposite else y_hi
        for other in range(2):
            from_core = 1 - ring if other else ring
            begin = (from_y * 2 * Z + from_z * 2 + from_core) * columns
            if halved:
                begin = begin + ring * rows
            copies.append(
                pltpu.make_async_copy(
                    source.at[other],
                    weight.at[pl.ds(pl.multiple_of(begin, 16), rows)],
                    sems.at[2 * number + other],
                )
            )
            copies[-1].start()
    return copies


def pack_kernel(places, heads, x_own, x_other, query, seat, *refs):
    count = len(places)
    piece_refs = refs[:count]
    part_out, unpack_query_out = refs[count : count + 2]
    weight, inputs, sems = refs[count + 2 :]
    width = query.shape[1]
    half_width = width // 2
    core = seat[2]
    copies = start_copies(places, piece_refs, seat, weight, sems)
    own_rows = x_own.shape[0]
    inputs[:own_rows] = x_own[...]
    inputs[own_rows:] = x_other[...]
    for copy in copies:
        copy.wait()
    base = pl.multiple_of(core * half_width, half_width)
    rows_in = inputs[...]
    keys = dot(weight[pl.ds(base, half_width)], rows_in, NT).astype(jnp.bfloat16)
    values = dot(weight[pl.ds(base + width, half_width)], rows_in, NT).astype(jnp.bfloat16)
    unpack_query_out[...] = dot(x_own[...], weight[2 * width :], NT).astype(jnp.bfloat16)
    scale = 1.0 / math.sqrt(DH)
    slots = query.shape[0]
    lanes = lax.broadcasted_iota(jnp.int32, (slots, STATS), 1)
    peaks = jnp.zeros((slots, STATS), jnp.float32)
    totals = jnp.zeros((slots, STATS), jnp.float32)
    query_half = query[:, pl.ds(base, half_width)]
    held = None
    for head in range(heads // 2):
        cols = slice(head * DH, (head + 1) * DH)
        scores = dot(query_half[:, cols], keys[cols], NN) * scale
        peak = jnp.max(scores, axis=1, keepdims=True)
        expo = jnp.exp(scores - peak)
        peaks = jnp.where(lanes == head, peak, peaks)
        totals = jnp.where(lanes == head, jnp.sum(expo, axis=1, keepdims=True), totals)
        numer = dot(expo.astype(jnp.bfloat16), values[cols], NT)
        if head % 2:
            both = jnp.concatenate([held, numer], axis=1).astype(jnp.bfloat16)
            part_out[:, (head - 1) * DH : (head + 1) * DH] = both
        held = numer
    room = heads // 2
    stats = jnp.zeros((slots, STATS), jnp.float32)
    number = 0
    for value, terms in ((peaks, 3), (totals, 2)):
        for _ in range(terms):
            term = value.astype(jnp.bfloat16).astype(jnp.float32)
            value = value - term
            stats = stats + (pltpu.roll(term, number * room, 1) if number else term)
            number += 1
    part_out[:, half_width:] = stats.astype(jnp.bfloat16)


def merge_kernel(heads, parts, gain, packed_out):
    count, slots, _ = parts.shape
    half_width = packed_out.shape[1] // 2
    room = heads // 2
    stats = parts[:, :, half_width:].astype(jnp.float32).reshape(count * slots, STATS)

    def term(number):
        return pltpu.roll(stats, STATS - number * room, 1) if number else stats

    peaks = (term(0) + term(1) + term(2)).reshape(count // 2, 2, slots, STATS)
    totals = (term(3) + term(4)).reshape(count // 2, 2, slots, STATS)
    lanes = lax.broadcasted_iota(jnp.int32, peaks.shape, 3)
    peaks = jnp.where(lanes < room, peaks, 0.0)
    factors = jnp.exp(peaks - jnp.max(peaks, axis=0, keepdims=True))
    total = jnp.sum(factors * totals, axis=0)
    spread_rows = lax.broadcasted_iota(jnp.int32, (STATS, half_width), 0)
    spread_cols = lax.broadcasted_iota(jnp.int32, (STATS, half_width), 1)
    spread = ((spread_cols // DH) == spread_rows).astype(jnp.float32)

    def spread_out(value):
        return lax.dot_general(
            value, spread, NN, precision=lax.Precision.HIGHEST, preferred_element_type=jnp.float32
        )

    wide = spread_out(factors.reshape(count * slots, STATS)).reshape(
        count // 2, 2, slots, half_width
    )
    numer = parts[:, :, :half_width].astype(jnp.float32).reshape(wide.shape)
    numer = jnp.sum(wide * numer, axis=0)
    wide_total = spread_out(total.reshape(2 * slots, STATS)).reshape(2, slots, half_width)
    ratio = numer / wide_total
    raw = jnp.concatenate([ratio[0], ratio[1]], axis=1)
    centred = raw - jnp.mean(raw, axis=1, keepdims=True)
    variance = jnp.mean(centred * centred, axis=1, keepdims=True)
    packed_out[...] = (centred * lax.rsqrt(variance + 1e-06) * gain[...]).astype(jnp.bfloat16)


def tail_kernel(places, heads, packed_a, packed_b, queries, pairing, seat, *refs):
    count = len(places)
    out, weight, attended, sems = refs[count:]
    width = queries.shape[1]
    copies = start_copies(places, refs[:count], seat, weight, sems)
    packed = jnp.concatenate([packed_a[...], packed_b[...]], axis=0)
    for copy in copies:
        copy.wait()
    keys = dot(weight[:width], packed, NT).astype(jnp.bfloat16)
    values = dot(packed, weight[width : 2 * width], NT).astype(jnp.bfloat16)
    scale = 1.0 / math.sqrt(DH)
    held = None
    for head in range(heads):
        cols = slice(head * DH, (head + 1) * DH)
        scores = dot(queries[:, cols], keys[cols], NN) * scale
        expo = jnp.exp(scores - jnp.max(scores, axis=1, keepdims=True))
        shares = (expo / jnp.sum(expo, axis=1, keepdims=True)).astype(jnp.bfloat16)
        result = dot(shares, values[:, cols], NN)
        if head % 2:
            both = jnp.concatenate([held, result], axis=1).astype(jnp.bfloat16)
            attended[:, (head - 1) * DH : (head + 1) * DH] = both
        held = result
    mixed = dot(attended[...], weight[2 * width :], NT)
    length = out.shape[0]
    reverse = mixed[length:]
    upper = reverse.astype(jnp.bfloat16)
    lower = (reverse - upper.astype(jnp.float32)).astype(jnp.bfloat16)
    paired = dot(upper, pairing[...], NN) + dot(lower, pairing[...], NN)
    out[...] = (mixed[:length] + paired).astype(jnp.bfloat16)


def params():
    return pltpu.CompilerParams(vmem_limit_bytes=VMEM_LIMIT)


VMEM = pl.BlockSpec(memory_space=pltpu.VMEM)
SMEM = pl.BlockSpec(memory_space=pltpu.SMEM)
ANY = pl.BlockSpec(memory_space=pl.ANY)


def shards(
    tokens,
    fwd_states,
    rev_states,
    conv_weight,
    embedding,
    in_weight,
    pack_query,
    pack_gain,
    tail_weight,
    channel_perm,
):
    local_len = tokens.shape[0]
    width = fwd_states.shape[1]
    slots = pack_query.shape[0]
    heads = width // DH
    count = lax.axis_size("seq")
    own_slots = slots // count
    place = lax.axis_index("seq")
    seat = jnp.stack([place // (2 * Z), place // 2 % Z, place % 2]).astype(jnp.int32)

    core = place % 2
    places, pieces = ring_pieces(in_weight.T, core)
    fwd_states, rev_states = after((fwd_states, rev_states), pieces[0])
    x_own = strand_inputs(tokens, fwd_states, rev_states, conv_weight, embedding)
    x_other = send(x_own, CORE_SWAP)
    pairing = (
        lax.broadcasted_iota(jnp.int32, (width, width), 0) == channel_perm[None, :]
    ).astype(jnp.bfloat16)
    tail_places, tail_pieces = ring_pieces(after(tail_weight.T, pieces[8]), core)

    part, queries = pl.pallas_call(
        functools.partial(pack_kernel, tuple(places), heads),
        out_shape=(
            jax.ShapeDtypeStruct((slots, width // 2 + STATS), jnp.bfloat16),
            jax.ShapeDtypeStruct((2 * local_len, width), jnp.bfloat16),
        ),
        in_specs=[VMEM, VMEM, VMEM, SMEM] + [ANY] * len(pieces),
        out_specs=(VMEM, VMEM),
        scratch_shapes=[
            pltpu.VMEM((3 * width, width), jnp.bfloat16),
            pltpu.VMEM((4 * local_len, width), jnp.bfloat16),
            pltpu.SemaphoreType.DMA((2 * len(pieces),)),
        ],
        compiler_params=params(),
        name="pack",
    )(x_own, x_other, pack_query, seat, *pieces)

    parts = lax.all_to_all(part.reshape(count, own_slots, -1), "seq", 0, 0)
    packed_own = pl.pallas_call(
        functools.partial(merge_kernel, heads),
        out_shape=jax.ShapeDtypeStruct((own_slots, width), jnp.bfloat16),
        in_specs=[VMEM, VMEM],
        out_specs=VMEM,
        compiler_params=params(),
        name="merge",
    )(parts, pack_gain[None, :])

    same_core = [list(range(core, count, 2)) for core in range(2)]
    copies = jnp.broadcast_to(packed_own[None], (count // 2, own_slots, width))
    packed_a = lax.all_to_all(copies, "seq", 0, 0, axis_index_groups=same_core)
    packed_a = packed_a.reshape(slots // 2, width)
    packed_b = send(packed_a, CORE_SWAP)

    return pl.pallas_call(
        functools.partial(tail_kernel, tuple(tail_places), heads),
        out_shape=jax.ShapeDtypeStruct((local_len, width), jnp.bfloat16),
        in_specs=[VMEM, VMEM, VMEM, VMEM, SMEM] + [ANY] * len(tail_pieces),
        out_specs=VMEM,
        scratch_shapes=[
            pltpu.VMEM((3 * width, width), jnp.bfloat16),
            pltpu.VMEM((2 * local_len, width), jnp.bfloat16),
            pltpu.SemaphoreType.DMA((2 * len(tail_pieces),)),
        ],
        compiler_params=params(),
        name="tail",
    )(packed_a, packed_b, queries, pairing, seat, *tail_pieces)


def solution(mesh):
    in_specs = (
        P(("batch", "seq")),
        P(("batch", "seq"), None),
        P(("batch", "seq"), None),
        P(),
        P(),
        P(None, "seq"),
        P(),
        P(),
        P(None, "seq"),
        P(),
    )
    out_specs = P(("batch", "seq"), None)
    return jax.shard_map(shards, mesh=mesh, in_specs=in_specs, out_specs=out_specs, check_vma=False)
```

```python
import functools
import math

import jax
import jax.numpy as jnp
from jax import lax
from jax.experimental import pallas as pl
from jax.experimental.pallas import tpu as pltpu
from jax.sharding import PartitionSpec as P

DH = 64
STATS = 128
MIB = 1024 * 1024
NT = (((1,), (1,)), ((), ()))
NN = (((1,), (0,)), ((), ()))

Z, X = 8, 4
AXES = ("seq", "batch")


def device_index(x, y, z, core):
    y_hi, y_lo = divmod(y % 4, 2)
    return (y_hi * 2 * Z + (z % Z) * 2 + core) * 2 * X + (x % X) * 2 + y_lo


def moves(target):
    return [
        (device_index(x, y, z, core), device_index(*target(x, y, z, core)))
        for x in range(X)
        for y in range(4)
        for z in range(Z)
        for core in range(2)
    ]


RING = moves(lambda x, y, z, core: (x, y, z + 1 - 2 * core, core))
Y_OPPOSITE = moves(lambda x, y, z, core: (x, 3 - y, z, core))
X_RING = moves(lambda x, y, z, core: (x + 1 - 2 * core, y, z, core))
CORE_SWAP = moves(lambda x, y, z, core: (x, y, z, 1 - core))


def send(shard, pairs):
    return lax.ppermute(shard, AXES, pairs)


def dot(a, b, dims):
    return lax.dot_general(a, b, dims, preferred_element_type=jnp.float32)


def as_column(row, backwards):
    length = row.shape[1]
    down = lax.broadcasted_iota(jnp.int32, (length, length), 0)
    across = lax.broadcasted_iota(jnp.int32, (length, length), 1)
    wanted = down + across == length - 1 if backwards else down == across
    return jnp.sum(jnp.where(wanted, row, 0.0), axis=1, keepdims=True)


def inputs_kernel(fwd, rev, rims, symbols, taps, embedding, rows_out):
    length = fwd.shape[0]
    for strand, states in enumerate((fwd, rev)):
        rim = rims[strand].astype(jnp.float32)
        extended = jnp.concatenate([rim, states[...].astype(jnp.float32)], axis=0)
        total = jnp.zeros(states.shape, jnp.float32)
        for lag in range(taps.shape[0]):
            begin = rim.shape[0] - lag
            total = total + taps[lag : lag + 1] * extended[begin : begin + length]
        hidden = total.astype(jnp.bfloat16).astype(jnp.float32)
        ids = as_column(symbols[strand : strand + 1], strand == 1)
        if strand == 1:
            ids = jnp.where(ids == 4.0, 4.0, 3.0 - ids)
        added = jnp.zeros(states.shape, jnp.float32)
        for symbol in range(embedding.shape[0]):
            row = embedding[symbol : symbol + 1]
            added = added + jnp.where(ids == float(symbol), row, 0.0)
        rows_out[strand * length : (strand + 1) * length] = (hidden + added).astype(jnp.bfloat16)


def strand_inputs(tokens, fwd_states, rev_states, conv_weight, embedding):
    local_len, width = fwd_states.shape
    count = lax.axis_size("seq")
    rims = jnp.stack([fwd_states[local_len - 8 :], rev_states[local_len - 8 :]])
    rims = lax.ppermute(rims, "seq", [(i, i + 1) for i in range(count - 1)])
    opposite = lax.ppermute(tokens, "seq", [(i, count - 1 - i) for i in range(count)])
    symbols = jnp.stack([tokens, opposite]).astype(jnp.float32)
    return pl.pallas_call(
        inputs_kernel,
        out_shape=jax.ShapeDtypeStruct((2 * local_len, width), jnp.bfloat16),
        in_specs=[VMEM] * 6,
        out_specs=VMEM,
        compiler_params=params(16),
        name="inputs",
    )(fwd_states, rev_states, rims, symbols, conv_weight, embedding)


def ring_step(held, step, core):
    last = step == Z // 2
    moved = []
    for halves, piece in held:
        if last:
            half = piece.shape[1] // 2
            piece = lax.dynamic_slice_in_dim(piece, core * half, half, 1)
        moved.append((halves, send(piece, RING)))
    own = [((halves, step, False, last), piece) for halves, piece in moved]
    swapped = [((halves, step, True, last), send(piece, CORE_SWAP)) for halves, piece in moved]
    return moved, own + swapped


def put_in_order(places, piece_refs, seat, weight, tail_part):
    y_hi, z, core = seat[0], seat[1], seat[2]
    columns = weight.shape[0] // 32
    width = weight.shape[1]
    for (halves, step, swapped, halved), source in zip(places, piece_refs):
        rows = source.shape[1]
        ring = 1 - core if swapped else core
        from_z = lax.rem(z + (2 * ring - 1) * step + Z, Z)
        for number in range(source.shape[0]):
            from_y = 1 - y_hi if halves[number // 2] else y_hi
            from_core = 1 - ring if number % 2 else ring
            begin = (from_y * 2 * Z + from_z * 2 + from_core) * columns
            if halved:
                begin = begin + ring * rows
            into = pl.ds(pl.multiple_of(begin, 16), rows)
            weight[into] = source[number, :, :width]
            tail_part[into] = source[number, :, width:]


def pack_kernel(places, heads, x_own, x_other, query, seat, *refs):
    count = len(places)
    piece_refs = refs[:count]
    part_out, queries_out, tail_out, weight, inputs, queries, tail_part, sems = refs[count:]
    own_rows = x_own.shape[0]
    width = x_own.shape[1]
    half_width = width // 2
    core = seat[2]
    put_in_order(places, piece_refs, seat, weight, tail_part)
    tail_store = pltpu.make_async_copy(tail_part, tail_out, sems.at[0])
    tail_store.start()
    inputs[:own_rows] = x_own[...]
    inputs[own_rows:] = x_other[...]
    base = pl.multiple_of(core * half_width, half_width)
    rows_in = inputs[...]
    keys = dot(weight[pl.ds(base, half_width)], rows_in, NT).astype(jnp.bfloat16)
    values = dot(weight[pl.ds(base + width, half_width)], rows_in, NT).astype(jnp.bfloat16)
    queries[...] = dot(x_own[...], weight[2 * width :], NT).astype(jnp.bfloat16)
    queries_store = pltpu.make_async_copy(queries, queries_out, sems.at[1])
    queries_store.start()
    scale = 1.0 / math.sqrt(DH)
    slots = query.shape[0]
    lanes = lax.broadcasted_iota(jnp.int32, (slots, STATS), 1)
    peaks = jnp.zeros((slots, STATS), jnp.float32)
    totals = jnp.zeros((slots, STATS), jnp.float32)
    query_half = query[:, pl.ds(base, half_width)]
    held = None
    for head in range(heads // 2):
        cols = slice(head * DH, (head + 1) * DH)
        scores = dot(query_half[:, cols], keys[cols], NN) * scale
        peak = jnp.max(scores, axis=1, keepdims=True)
        expo = jnp.exp(scores - peak)
        peaks = jnp.where(lanes == head, peak, peaks)
        totals = jnp.where(lanes == head, jnp.sum(expo, axis=1, keepdims=True), totals)
        numer = dot(expo.astype(jnp.bfloat16), values[cols], NT)
        if head % 2:
            both = jnp.concatenate([held, numer], axis=1).astype(jnp.bfloat16)
            part_out[:, (head - 1) * DH : (head + 1) * DH] = both
        held = numer
    room = heads // 2
    stats = jnp.zeros((slots, STATS), jnp.float32)
    number = 0
    for value, terms in ((peaks, 3), (totals, 2)):
        for _ in range(terms):
            term = value.astype(jnp.bfloat16).astype(jnp.float32)
            value = value - term
            stats = stats + (pltpu.roll(term, number * room, 1) if number else term)
            number += 1
    part_out[:, half_width:] = stats.astype(jnp.bfloat16)
    tail_store.wait()
    queries_store.wait()


def merge_kernel(heads, parts, gain, packed_out):
    count, slots, _ = parts.shape
    half_width = packed_out.shape[1] // 2
    room = heads // 2
    stats = parts[:, :, half_width:].astype(jnp.float32).reshape(count * slots, STATS)

    def term(number):
        return pltpu.roll(stats, STATS - number * room, 1) if number else stats

    peaks = (term(0) + term(1) + term(2)).reshape(count // 2, 2, slots, STATS)
    totals = (term(3) + term(4)).reshape(count // 2, 2, slots, STATS)
    lanes = lax.broadcasted_iota(jnp.int32, peaks.shape, 3)
    peaks = jnp.where(lanes < room, peaks, 0.0)
    factors = jnp.exp(peaks - jnp.max(peaks, axis=0, keepdims=True))
    total = jnp.sum(factors * totals, axis=0)
    spread_rows = lax.broadcasted_iota(jnp.int32, (STATS, half_width), 0)
    spread_cols = lax.broadcasted_iota(jnp.int32, (STATS, half_width), 1)
    spread = ((spread_cols // DH) == spread_rows).astype(jnp.float32)

    def spread_out(value):
        return lax.dot_general(
            value, spread, NN, precision=lax.Precision.HIGHEST, preferred_element_type=jnp.float32
        )

    wide = spread_out(factors.reshape(count * slots, STATS)).reshape(
        count // 2, 2, slots, half_width
    )
    numer = parts[:, :, :half_width].astype(jnp.float32).reshape(wide.shape)
    numer = jnp.sum(wide * numer, axis=0)
    wide_total = spread_out(total.reshape(2 * slots, STATS)).reshape(2, slots, half_width)
    ratio = numer / wide_total
    raw = jnp.concatenate([ratio[0], ratio[1]], axis=1)
    centred = raw - jnp.mean(raw, axis=1, keepdims=True)
    variance = jnp.mean(centred * centred, axis=1, keepdims=True)
    packed_out[...] = (centred * lax.rsqrt(variance + 1e-06) * gain[...]).astype(jnp.bfloat16)


def tail_kernel(heads, packed_a, packed_b, query_fwd, query_rev, pairing, seat, *refs):
    own, near, near_swapped, far, far_swapped, out, queries, weight, attended = refs
    width = queries.shape[1]
    length = out.shape[0]
    x, core = seat[3], seat[2]
    block = width // X
    half = weight.shape[0] // 2

    def columns(number):
        return pl.ds(pl.multiple_of(lax.rem(number + X, X) * block, block), block)

    weight[:, columns(x)] = own[...]
    weight[:, columns(x + 2 * core - 1)] = near[...]
    weight[:, columns(x + 1 - 2 * core)] = near_swapped[...]
    weight[pl.ds(pl.multiple_of(core * half, half), half), columns(x + 2)] = far[...]
    weight[pl.ds(pl.multiple_of((1 - core) * half, half), half), columns(x + 2)] = far_swapped[...]
    queries[:length] = query_fwd[:length]
    queries[length:] = query_rev[...]
    packed = jnp.concatenate([packed_a[...], packed_b[...]], axis=0)
    keys = dot(weight[:width], packed, NT).astype(jnp.bfloat16)
    values = dot(packed, weight[width : 2 * width], NT).astype(jnp.bfloat16)
    scale = 1.0 / math.sqrt(DH)
    held = None
    for head in range(heads):
        cols = slice(head * DH, (head + 1) * DH)
        scores = dot(queries[:, cols], keys[cols], NN) * scale
        expo = jnp.exp(scores - jnp.max(scores, axis=1, keepdims=True))
        shares = (expo / jnp.sum(expo, axis=1, keepdims=True)).astype(jnp.bfloat16)
        result = dot(shares, values[:, cols], NN)
        if head % 2:
            both = jnp.concatenate([held, result], axis=1).astype(jnp.bfloat16)
            attended[:, (head - 1) * DH : (head + 1) * DH] = both
        held = result
    order = lax.broadcasted_iota(jnp.int32, (length, length), 0)
    order = order + lax.broadcasted_iota(jnp.int32, (length, length), 1) == length - 1
    flipped = dot(order.astype(jnp.bfloat16), attended[length:], NN).astype(jnp.bfloat16)
    attended[length:] = flipped
    mixed = dot(attended[...], weight[2 * width :], NT)
    reverse = mixed[length:]
    upper = reverse.astype(jnp.bfloat16)
    lower = (reverse - upper.astype(jnp.float32)).astype(jnp.bfloat16)
    paired = dot(upper, pairing[...], NN) + dot(lower, pairing[...], NN)
    out[...] = (mixed[:length] + paired).astype(jnp.bfloat16)


def params(mib):
    return pltpu.CompilerParams(vmem_limit_bytes=mib * MIB)


VMEM = pl.BlockSpec(memory_space=pltpu.VMEM)
HBM = pl.BlockSpec(memory_space=pltpu.HBM)
SMEM = pl.BlockSpec(memory_space=pltpu.SMEM)


def shards(
    tokens,
    fwd_states,
    rev_states,
    conv_weight,
    embedding,
    in_weight,
    pack_query,
    pack_gain,
    tail_weight,
    channel_perm,
):
    local_len = tokens.shape[0]
    width = fwd_states.shape[1]
    slots = pack_query.shape[0]
    heads = width // DH
    count = lax.axis_size("seq")
    own_slots = slots // count
    place = lax.axis_index("seq")
    x = lax.axis_index("batch") // 2
    core = place % 2
    seat = jnp.stack([place // (2 * Z), place // 2 % Z, core, x]).astype(jnp.int32)

    block = width // X
    tail_block = lax.dynamic_slice_in_dim(tail_weight.T, x * block, block, 1)
    shard = jnp.concatenate([in_weight.T, tail_block], axis=1)
    across = send(shard, Y_OPPOSITE)
    held = [
        ((number,), jnp.stack([mine, send(mine, CORE_SWAP)]))
        for number, mine in enumerate((shard, across))
    ]
    pieces = [((halves, 0, False, False), piece) for halves, piece in held]
    x_own = strand_inputs(tokens, fwd_states, rev_states, conv_weight, embedding)
    pairing = (
        lax.broadcasted_iota(jnp.int32, (width, width), 0) == channel_perm[None, :]
    ).astype(jnp.bfloat16)
    x_own, pairing = lax.optimization_barrier((x_own, pairing))
    x_other = send(x_own, CORE_SWAP)
    for step in range(1, Z // 2 + 1):
        held, brought = ring_step(held, step, core)
        pieces += brought
    places, pieces = zip(*pieces)

    part, queries, own = pl.pallas_call(
        functools.partial(pack_kernel, places, heads),
        out_shape=(
            jax.ShapeDtypeStruct((slots, width // 2 + STATS), jnp.bfloat16),
            pltpu.HBM((2 * local_len, width), jnp.bfloat16),
            pltpu.HBM((3 * width, block), jnp.bfloat16),
        ),
        in_specs=[VMEM, VMEM, VMEM, SMEM] + [VMEM] * len(pieces),
        out_specs=(VMEM, HBM, HBM),
        scratch_shapes=[
            pltpu.VMEM((3 * width, width), jnp.bfloat16),
            pltpu.VMEM((4 * local_len, width), jnp.bfloat16),
            pltpu.VMEM((2 * local_len, width), jnp.bfloat16),
            pltpu.VMEM((3 * width, block), jnp.bfloat16),
            pltpu.SemaphoreType.DMA((2,)),
        ],
        compiler_params=params(20),
        name="pack",
    )(x_own, x_other, pack_query, seat, *pieces)

    near = send(own, X_RING)
    parts = lax.all_to_all(part.reshape(count, own_slots, -1), "seq", 0, 0)
    parts, near = lax.optimization_barrier((parts, near))
    mirror = [(i, count - 1 - i) for i in range(count)]
    query_rev = lax.ppermute(queries[local_len:], "seq", mirror)
    near_swapped = send(near, CORE_SWAP)
    half = 3 * width // 2
    far = send(lax.dynamic_slice_in_dim(near, core * half, half, 0), X_RING)
    packed_own = pl.pallas_call(
        functools.partial(merge_kernel, heads),
        out_shape=jax.ShapeDtypeStruct((own_slots, width), jnp.bfloat16),
        in_specs=[VMEM, VMEM],
        out_specs=VMEM,
        compiler_params=params(12),
        name="merge",
    )(parts, pack_gain[None, :])

    same_core = [list(range(core, count, 2)) for core in range(2)]
    copies = jnp.broadcast_to(packed_own[None], (count // 2, own_slots, width))
    packed_a = lax.all_to_all(copies, "seq", 0, 0, axis_index_groups=same_core)
    packed_a = packed_a.reshape(slots // 2, width)
    packed_a, far, near_swapped, query_rev = lax.optimization_barrier(
        (packed_a, far, near_swapped, query_rev)
    )
    packed_b = send(packed_a, CORE_SWAP)
    far_swapped = send(far, CORE_SWAP)

    return pl.pallas_call(
        functools.partial(tail_kernel, heads),
        out_shape=jax.ShapeDtypeStruct((local_len, width), jnp.bfloat16),
        in_specs=[VMEM] * 5 + [SMEM] + [VMEM] * 5,
        out_specs=VMEM,
        scratch_shapes=[
            pltpu.VMEM((2 * local_len, width), jnp.bfloat16),
            pltpu.VMEM((3 * width, width), jnp.bfloat16),
            pltpu.VMEM((2 * local_len, width), jnp.bfloat16),
        ],
        compiler_params=params(20),
        name="tail",
    )(
        packed_a,
        packed_b,
        queries,
        query_rev,
        pairing,
        seat,
        own,
        near,
        near_swapped,
        far,
        far_swapped,
    )


def solution(mesh):
    in_specs = (
        P(("batch", "seq")),
        P(("batch", "seq"), None),
        P(("batch", "seq"), None),
        P(),
        P(),
        P(None, "seq"),
        P(),
        P(),
        P(None, "seq"),
        P(),
    )
    out_specs = P(("batch", "seq"), None)
    return jax.shard_map(shards, mesh=mesh, in_specs=in_specs, out_specs=out_specs, check_vma=False)
```

```python
import functools
import math

import jax
import jax.numpy as jnp
from jax import lax
from jax.experimental import pallas as pl
from jax.experimental.pallas import tpu as pltpu
from jax.sharding import PartitionSpec as P

DH = 64
STATS = 128
MIB = 1024 * 1024
NT = (((1,), (1,)), ((), ()))
NN = (((1,), (0,)), ((), ()))

Z, X = 8, 4
AXES = ("seq", "batch")


def device_index(x, y, z, core):
    y_hi, y_lo = divmod(y % 4, 2)
    return (y_hi * 2 * Z + (z % Z) * 2 + core) * 2 * X + (x % X) * 2 + y_lo


def moves(target):
    return [
        (device_index(x, y, z, core), device_index(*target(x, y, z, core)))
        for x in range(X)
        for y in range(4)
        for z in range(Z)
        for core in range(2)
    ]


RING = moves(lambda x, y, z, core: (x, y, z + 1 - 2 * core, core))
Y_OPPOSITE = moves(lambda x, y, z, core: (x, 3 - y, z, core))
X_RING = moves(lambda x, y, z, core: (x + 1 - 2 * core, y, z, core))
CORE_SWAP = moves(lambda x, y, z, core: (x, y, z, 1 - core))


def send(shard, pairs):
    return lax.ppermute(shard, AXES, pairs)


def dot(a, b, dims):
    return lax.dot_general(a, b, dims, preferred_element_type=jnp.float32)


def as_column(row, backwards):
    length = row.shape[1]
    down = lax.broadcasted_iota(jnp.int32, (length, length), 0)
    across = lax.broadcasted_iota(jnp.int32, (length, length), 1)
    wanted = down + across == length - 1 if backwards else down == across
    return jnp.sum(jnp.where(wanted, row, 0.0), axis=1, keepdims=True)


def inputs_kernel(fwd, rev, rims, symbols, taps, embedding, rows_out):
    length = fwd.shape[0]
    for strand, states in enumerate((fwd, rev)):
        rim = rims[strand].astype(jnp.float32)
        extended = jnp.concatenate([rim, states[...].astype(jnp.float32)], axis=0)
        total = jnp.zeros(states.shape, jnp.float32)
        for lag in range(taps.shape[0]):
            begin = rim.shape[0] - lag
            total = total + taps[lag : lag + 1] * extended[begin : begin + length]
        hidden = total.astype(jnp.bfloat16).astype(jnp.float32)
        ids = as_column(symbols[strand : strand + 1], strand == 1)
        if strand == 1:
            ids = jnp.where(ids == 4.0, 4.0, 3.0 - ids)
        added = jnp.zeros(states.shape, jnp.float32)
        for symbol in range(embedding.shape[0]):
            row = embedding[symbol : symbol + 1]
            added = added + jnp.where(ids == float(symbol), row, 0.0)
        rows_out[strand * length : (strand + 1) * length] = (hidden + added).astype(jnp.bfloat16)


def strand_inputs(tokens, fwd_states, rev_states, conv_weight, embedding):
    local_len, width = fwd_states.shape
    count = lax.axis_size("seq")
    rims = jnp.stack([fwd_states[local_len - 8 :], rev_states[local_len - 8 :]])
    rims = lax.ppermute(rims, "seq", [(i, i + 1) for i in range(count - 1)])
    opposite = lax.ppermute(tokens, "seq", [(i, count - 1 - i) for i in range(count)])
    symbols = jnp.stack([tokens, opposite]).astype(jnp.float32)
    return pl.pallas_call(
        inputs_kernel,
        out_shape=jax.ShapeDtypeStruct((2 * local_len, width), jnp.bfloat16),
        in_specs=[VMEM] * 6,
        out_specs=VMEM,
        compiler_params=params(16),
        name="inputs",
    )(fwd_states, rev_states, rims, symbols, conv_weight, embedding)


def ring_step(held, step, core):
    last = step == Z // 2
    moved = []
    for halves, piece in held:
        if last:
            half = piece.shape[1] // 2
            piece = lax.dynamic_slice_in_dim(piece, core * half, half, 1)
        moved.append((halves, send(piece, RING)))
    own = [((halves, step, False, last), piece) for halves, piece in moved]
    swapped = [((halves, step, True, last), send(piece, CORE_SWAP)) for halves, piece in moved]
    return moved, own + swapped


def put_in_order(places, piece_refs, seat, weight, tail_part):
    y_hi, z, core = seat[0], seat[1], seat[2]
    columns = weight.shape[0] // 32
    width = weight.shape[1]
    for (halves, step, swapped, halved), source in zip(places, piece_refs):
        rows = source.shape[1]
        ring = 1 - core if swapped else core
        from_z = lax.rem(z + (2 * ring - 1) * step + Z, Z)
        for number in range(source.shape[0]):
            from_y = 1 - y_hi if halves[number // 2] else y_hi
            from_core = 1 - ring if number % 2 else ring
            begin = (from_y * 2 * Z + from_z * 2 + from_core) * columns
            if halved:
                begin = begin + ring * rows
            into = pl.ds(pl.multiple_of(begin, 16), rows)
            weight[into] = source[number, :, :width]
            tail_part[into] = source[number, :, width:]


def pack_kernel(places, heads, x_own, x_other, query, seat, *refs):
    count = len(places)
    piece_refs = refs[:count]
    part_out, query_fwd, query_rev, tail_part, weight, inputs = refs[count:]
    own_rows = x_own.shape[0]
    width = x_own.shape[1]
    half_width = width // 2
    core = seat[2]
    put_in_order(places, piece_refs, seat, weight, tail_part)
    inputs[:own_rows] = x_own[...]
    inputs[own_rows:] = x_other[...]
    base = pl.multiple_of(core * half_width, half_width)
    rows_in = inputs[...]
    keys = dot(weight[pl.ds(base, half_width)], rows_in, NT).astype(jnp.bfloat16)
    values = dot(weight[pl.ds(base + width, half_width)], rows_in, NT).astype(jnp.bfloat16)
    queries = dot(x_own[...], weight[2 * width :], NT).astype(jnp.bfloat16)
    query_fwd[...] = queries[: own_rows // 2]
    query_rev[...] = queries[own_rows // 2 :]
    scale = 1.0 / math.sqrt(DH)
    slots = query.shape[0]
    lanes = lax.broadcasted_iota(jnp.int32, (slots, STATS), 1)
    peaks = jnp.zeros((slots, STATS), jnp.float32)
    totals = jnp.zeros((slots, STATS), jnp.float32)
    query_half = query[:, pl.ds(base, half_width)]
    held = None
    for head in range(heads // 2):
        cols = slice(head * DH, (head + 1) * DH)
        scores = dot(query_half[:, cols], keys[cols], NN) * scale
        peak = jnp.max(scores, axis=1, keepdims=True)
        expo = jnp.exp(scores - peak)
        peaks = jnp.where(lanes == head, peak, peaks)
        totals = jnp.where(lanes == head, jnp.sum(expo, axis=1, keepdims=True), totals)
        numer = dot(expo.astype(jnp.bfloat16), values[cols], NT)
        if head % 2:
            both = jnp.concatenate([held, numer], axis=1).astype(jnp.bfloat16)
            part_out[:, (head - 1) * DH : (head + 1) * DH] = both
        held = numer
    room = heads // 2
    stats = jnp.zeros((slots, STATS), jnp.float32)
    number = 0
    for value, terms in ((peaks, 3), (totals, 2)):
        for _ in range(terms):
            term = value.astype(jnp.bfloat16).astype(jnp.float32)
            value = value - term
            stats = stats + (pltpu.roll(term, number * room, 1) if number else term)
            number += 1
    part_out[:, half_width:] = stats.astype(jnp.bfloat16)


def merge_kernel(heads, parts, gain, packed_out):
    count, slots, _ = parts.shape
    half_width = packed_out.shape[2] // 2
    room = heads // 2
    stats = parts[:, :, half_width:].astype(jnp.float32).reshape(count * slots, STATS)

    def term(number):
        return pltpu.roll(stats, STATS - number * room, 1) if number else stats

    peaks = (term(0) + term(1) + term(2)).reshape(count // 2, 2, slots, STATS)
    totals = (term(3) + term(4)).reshape(count // 2, 2, slots, STATS)
    lanes = lax.broadcasted_iota(jnp.int32, peaks.shape, 3)
    peaks = jnp.where(lanes < room, peaks, 0.0)
    factors = jnp.exp(peaks - jnp.max(peaks, axis=0, keepdims=True))
    total = jnp.sum(factors * totals, axis=0)
    spread_rows = lax.broadcasted_iota(jnp.int32, (STATS, half_width), 0)
    spread_cols = lax.broadcasted_iota(jnp.int32, (STATS, half_width), 1)
    spread = ((spread_cols // DH) == spread_rows).astype(jnp.float32)

    def spread_out(value):
        return lax.dot_general(
            value, spread, NN, precision=lax.Precision.HIGHEST, preferred_element_type=jnp.float32
        )

    wide = spread_out(factors.reshape(count * slots, STATS)).reshape(
        count // 2, 2, slots, half_width
    )
    numer = parts[:, :, :half_width].astype(jnp.float32).reshape(wide.shape)
    numer = jnp.sum(wide * numer, axis=0)
    wide_total = spread_out(total.reshape(2 * slots, STATS)).reshape(2, slots, half_width)
    ratio = numer / wide_total
    raw = jnp.concatenate([ratio[0], ratio[1]], axis=1)
    centred = raw - jnp.mean(raw, axis=1, keepdims=True)
    variance = jnp.mean(centred * centred, axis=1, keepdims=True)
    packed = (centred * lax.rsqrt(variance + 1e-06) * gain[...]).astype(jnp.bfloat16)
    packed_out[...] = jnp.broadcast_to(packed[None], packed_out.shape)


def tail_kernel(heads, packed_a, packed_b, query_fwd, query_rev, pairing, seat, *refs):
    own, near, near_swapped, far, far_swapped, out, queries, weight, attended = refs
    width = queries.shape[1]
    length = out.shape[0]
    x, core = seat[3], seat[2]
    block = width // X
    half = weight.shape[0] // 2

    def columns(number):
        return pl.ds(pl.multiple_of(lax.rem(number + X, X) * block, block), block)

    weight[:, columns(x)] = own[...]
    weight[:, columns(x + 2 * core - 1)] = near[...]
    weight[:, columns(x + 1 - 2 * core)] = near_swapped[...]
    weight[pl.ds(pl.multiple_of(core * half, half), half), columns(x + 2)] = far[...]
    weight[pl.ds(pl.multiple_of((1 - core) * half, half), half), columns(x + 2)] = far_swapped[...]
    queries[:length] = query_fwd[...]
    queries[length:] = query_rev[...]
    packed = jnp.concatenate([packed_a[...], packed_b[...]], axis=0)
    keys = dot(weight[:width], packed, NT).astype(jnp.bfloat16)
    values = dot(packed, weight[width : 2 * width], NT).astype(jnp.bfloat16)
    scale = 1.0 / math.sqrt(DH)
    held = None
    for head in range(heads):
        cols = slice(head * DH, (head + 1) * DH)
        scores = dot(queries[:, cols], keys[cols], NN) * scale
        expo = jnp.exp(scores - jnp.max(scores, axis=1, keepdims=True))
        shares = (expo / jnp.sum(expo, axis=1, keepdims=True)).astype(jnp.bfloat16)
        result = dot(shares, values[:, cols], NN)
        if head % 2:
            both = jnp.concatenate([held, result], axis=1).astype(jnp.bfloat16)
            attended[:, (head - 1) * DH : (head + 1) * DH] = both
        held = result
    order = lax.broadcasted_iota(jnp.int32, (length, length), 0)
    order = order + lax.broadcasted_iota(jnp.int32, (length, length), 1) == length - 1
    flipped = dot(order.astype(jnp.bfloat16), attended[length:], NN).astype(jnp.bfloat16)
    attended[length:] = flipped
    mixed = dot(attended[...], weight[2 * width :], NT)
    reverse = mixed[length:]
    upper = reverse.astype(jnp.bfloat16)
    lower = (reverse - upper.astype(jnp.float32)).astype(jnp.bfloat16)
    paired = dot(upper, pairing[...], NN) + dot(lower, pairing[...], NN)
    out[...] = (mixed[:length] + paired).astype(jnp.bfloat16)


def params(mib):
    return pltpu.CompilerParams(vmem_limit_bytes=mib * MIB)


VMEM = pl.BlockSpec(memory_space=pltpu.VMEM)
SMEM = pl.BlockSpec(memory_space=pltpu.SMEM)


def shards(
    tokens,
    fwd_states,
    rev_states,
    conv_weight,
    embedding,
    in_weight,
    pack_query,
    pack_gain,
    tail_weight,
    channel_perm,
):
    local_len = tokens.shape[0]
    width = fwd_states.shape[1]
    slots = pack_query.shape[0]
    heads = width // DH
    count = lax.axis_size("seq")
    own_slots = slots // count
    place = lax.axis_index("seq")
    x = lax.axis_index("batch") // 2
    core = place % 2
    seat = jnp.stack([place // (2 * Z), place // 2 % Z, core, x]).astype(jnp.int32)

    block = width // X
    tail_block = lax.dynamic_slice_in_dim(tail_weight.T, x * block, block, 1)
    shard = jnp.concatenate([in_weight.T, tail_block], axis=1)
    across = send(shard, Y_OPPOSITE)
    held = [
        ((number,), jnp.stack([mine, send(mine, CORE_SWAP)]))
        for number, mine in enumerate((shard, across))
    ]
    pieces = [((halves, 0, False, False), piece) for halves, piece in held]
    x_own = strand_inputs(tokens, fwd_states, rev_states, conv_weight, embedding)
    pairing = (
        lax.broadcasted_iota(jnp.int32, (width, width), 0) == channel_perm[None, :]
    ).astype(jnp.bfloat16)
    x_own, pairing = lax.optimization_barrier((x_own, pairing))
    x_other = send(x_own, CORE_SWAP)
    for step in range(1, Z // 2 + 1):
        held, brought = ring_step(held, step, core)
        pieces += brought
    places, pieces = zip(*pieces)

    part, query_fwd, query_rev, own = pl.pallas_call(
        functools.partial(pack_kernel, places, heads),
        out_shape=(
            jax.ShapeDtypeStruct((slots, width // 2 + STATS), jnp.bfloat16),
            jax.ShapeDtypeStruct((local_len, width), jnp.bfloat16),
            jax.ShapeDtypeStruct((local_len, width), jnp.bfloat16),
            jax.ShapeDtypeStruct((3 * width, block), jnp.bfloat16),
        ),
        in_specs=[VMEM, VMEM, VMEM, SMEM] + [VMEM] * len(pieces),
        out_specs=(VMEM,) * 4,
        scratch_shapes=[
            pltpu.VMEM((3 * width, width), jnp.bfloat16),
            pltpu.VMEM((4 * local_len, width), jnp.bfloat16),
        ],
        compiler_params=params(20),
        name="pack",
    )(x_own, x_other, pack_query, seat, *pieces)

    near = send(own, X_RING)
    mirror = [(i, count - 1 - i) for i in range(count)]
    query_rev = lax.ppermute(query_rev, "seq", mirror)
    rounds = 1 + (channel_perm[0] >> 31)
    _, parts = lax.while_loop(
        lambda state: state[0] < rounds,
        lambda state: (state[0] + 1, lax.all_to_all(state[1], "seq", 0, 0)),
        (jnp.int32(0), part.reshape(count, own_slots, -1)),
    )
    parts, near, query_rev = lax.optimization_barrier((parts, near, query_rev))
    near_swapped = send(near, CORE_SWAP)
    half = 3 * width // 2
    far = send(lax.dynamic_slice_in_dim(near, core * half, half, 0), X_RING)
    copies = pl.pallas_call(
        functools.partial(merge_kernel, heads),
        out_shape=jax.ShapeDtypeStruct((count // 2, own_slots, width), jnp.bfloat16),
        in_specs=[VMEM, VMEM],
        out_specs=VMEM,
        compiler_params=params(12),
        name="merge",
    )(parts, pack_gain[None, :])

    same_core = [list(range(core, count, 2)) for core in range(2)]
    packed_a = lax.all_to_all(copies, "seq", 0, 0, axis_index_groups=same_core)
    packed_a = packed_a.reshape(slots // 2, width)
    packed_a, far, near_swapped = lax.optimization_barrier((packed_a, far, near_swapped))
    packed_b = send(packed_a, CORE_SWAP)
    far_swapped = send(far, CORE_SWAP)

    return pl.pallas_call(
        functools.partial(tail_kernel, heads),
        out_shape=jax.ShapeDtypeStruct((local_len, width), jnp.bfloat16),
        in_specs=[VMEM] * 5 + [SMEM] + [VMEM] * 5,
        out_specs=VMEM,
        scratch_shapes=[
            pltpu.VMEM((2 * local_len, width), jnp.bfloat16),
            pltpu.VMEM((3 * width, width), jnp.bfloat16),
            pltpu.VMEM((2 * local_len, width), jnp.bfloat16),
        ],
        compiler_params=params(20),
        name="tail",
    )(
        packed_a,
        packed_b,
        query_fwd,
        query_rev,
        pairing,
        seat,
        own,
        near,
        near_swapped,
        far,
        far_swapped,
    )


def solution(mesh):
    in_specs = (
        P(("batch", "seq")),
        P(("batch", "seq"), None),
        P(("batch", "seq"), None),
        P(),
        P(),
        P(None, "seq"),
        P(),
        P(),
        P(None, "seq"),
        P(),
    )
    out_specs = P(("batch", "seq"), None)
    return jax.shard_map(shards, mesh=mesh, in_specs=in_specs, out_specs=out_specs, check_vma=False)
```

```python
import functools
import math

import jax
import jax.numpy as jnp
from jax import lax
from jax.experimental import pallas as pl
from jax.experimental.pallas import tpu as pltpu
from jax.sharding import PartitionSpec as P

DH = 64
STATS = 128
SCALE = 1.0 / math.sqrt(DH)
MIB = 1024 * 1024
NT = (((1,), (1,)), ((), ()))
NN = (((1,), (0,)), ((), ()))

Z, X = 8, 4
AXES = ("seq", "batch")


def device_index(x, y, z, core):
    y_hi, y_lo = divmod(y % 4, 2)
    return (y_hi * 2 * Z + (z % Z) * 2 + core) * 2 * X + (x % X) * 2 + y_lo


def moves(target):
    return [
        (device_index(x, y, z, core), device_index(*target(x, y, z, core)))
        for x in range(X)
        for y in range(4)
        for z in range(Z)
        for core in range(2)
    ]


RING = moves(lambda x, y, z, core: (x, y, z + 1 - 2 * core, core))
Y_OPPOSITE = moves(lambda x, y, z, core: (x, 3 - y, z, core))
X_RING = moves(lambda x, y, z, core: (x + 1 - 2 * core, y, z, core))
CORE_SWAP = moves(lambda x, y, z, core: (x, y, z, 1 - core))


def send(shard, pairs):
    return lax.ppermute(shard, AXES, pairs)


def dot(a, b, dims):
    return lax.dot_general(a, b, dims, preferred_element_type=jnp.float32)


def as_column(row, backwards):
    length = row.shape[1]
    down = lax.broadcasted_iota(jnp.int32, (length, length), 0)
    across = lax.broadcasted_iota(jnp.int32, (length, length), 1)
    wanted = down + across == length - 1 if backwards else down == across
    return jnp.sum(jnp.where(wanted, row, 0.0), axis=1, keepdims=True)


def inputs_kernel(fwd, rev, rims, symbols, taps, embedding, rows_out):
    length = fwd.shape[0]
    for strand, states in enumerate((fwd, rev)):
        rim = rims[strand].astype(jnp.float32)
        extended = jnp.concatenate([rim, states[...].astype(jnp.float32)], axis=0)
        total = jnp.zeros(states.shape, jnp.float32)
        for lag in range(taps.shape[0]):
            begin = rim.shape[0] - lag
            total = total + taps[lag : lag + 1] * extended[begin : begin + length]
        hidden = total.astype(jnp.bfloat16).astype(jnp.float32)
        ids = as_column(symbols[strand : strand + 1], strand == 1)
        if strand == 1:
            ids = jnp.where(ids == 4.0, 4.0, 3.0 - ids)
        added = jnp.zeros(states.shape, jnp.float32)
        for symbol in range(embedding.shape[0]):
            row = embedding[symbol : symbol + 1]
            added = added + jnp.where(ids == float(symbol), row, 0.0)
        rows_out[strand * length : (strand + 1) * length] = (hidden + added).astype(jnp.bfloat16)


def strand_inputs(tokens, fwd_states, rev_states, conv_weight, embedding):
    local_len, width = fwd_states.shape
    count = lax.axis_size("seq")
    rims = jnp.stack([fwd_states[local_len - 8 :], rev_states[local_len - 8 :]])
    rims = lax.ppermute(rims, "seq", [(i, i + 1) for i in range(count - 1)])
    opposite = lax.ppermute(tokens, "seq", [(i, count - 1 - i) for i in range(count)])
    symbols = jnp.stack([tokens, opposite]).astype(jnp.float32)
    return pl.pallas_call(
        inputs_kernel,
        out_shape=jax.ShapeDtypeStruct((2 * local_len, width), jnp.bfloat16),
        in_specs=[VMEM] * 6,
        out_specs=VMEM,
        compiler_params=params(16),
        name="inputs",
    )(fwd_states, rev_states, rims, symbols, conv_weight, embedding)


def ring_step(held, step, core):
    last = step == Z // 2
    moved = []
    for halves, piece in held:
        if last:
            half = piece.shape[1] // 2
            piece = lax.dynamic_slice_in_dim(piece, core * half, half, 1)
        moved.append((halves, send(piece, RING)))
    own = [((halves, step, False, last), piece) for halves, piece in moved]
    swapped = [((halves, step, True, last), send(piece, CORE_SWAP)) for halves, piece in moved]
    return moved, own + swapped


def put_in_order(places, piece_refs, seat, weight, tail_part):
    y_hi, z, core = seat[0], seat[1], seat[2]
    columns = weight.shape[0] // 32
    width = weight.shape[1]
    for (halves, step, swapped, halved), source in zip(places, piece_refs):
        rows = source.shape[1]
        ring = 1 - core if swapped else core
        from_z = lax.rem(z + (2 * ring - 1) * step + Z, Z)
        for number in range(source.shape[0]):
            from_y = 1 - y_hi if halves[number // 2] else y_hi
            from_core = 1 - ring if number % 2 else ring
            begin = (from_y * 2 * Z + from_z * 2 + from_core) * columns
            if halved:
                begin = begin + ring * rows
            into = pl.ds(pl.multiple_of(begin, 16), rows)
            weight[into] = source[number, :, :width]
            tail_part[into] = source[number, :, width:]


def pack_kernel(places, heads, x_own, x_other, query, seat, *refs):
    count = len(places)
    piece_refs = refs[:count]
    part_out, query_fwd, query_rev, tail_part, weight, inputs = refs[count:]
    own_rows = x_own.shape[0]
    width = x_own.shape[1]
    half_width = width // 2
    core = seat[2]
    put_in_order(places, piece_refs, seat, weight, tail_part)
    inputs[:own_rows] = x_own[...]
    inputs[own_rows:] = x_other[...]
    base = pl.multiple_of(core * half_width, half_width)
    rows_in = inputs[...]
    keys = dot(weight[pl.ds(base, half_width)], rows_in, NT).astype(jnp.bfloat16)
    values = dot(weight[pl.ds(base + width, half_width)], rows_in, NT).astype(jnp.bfloat16)
    queries = dot(x_own[...], weight[2 * width :], NT).astype(jnp.bfloat16)
    query_fwd[...] = queries[: own_rows // 2]
    query_rev[...] = queries[own_rows // 2 :]
    slots = query.shape[0]
    lanes = lax.broadcasted_iota(jnp.int32, (slots, STATS), 1)
    rows = lax.broadcasted_iota(jnp.int32, (2 * DH, inputs.shape[0]), 0)
    peaks = jnp.zeros((slots, STATS), jnp.float32)
    totals = jnp.zeros((slots, STATS), jnp.float32)
    query_half = query[:, pl.ds(base, half_width)] * SCALE
    for pair in range(heads // 4):
        cols = slice(pair * 2 * DH, (pair + 1) * 2 * DH)
        results = []
        for number in range(2):
            head = 2 * pair + number
            mine = lanes // DH == number
            scores = dot(jnp.where(mine, query_half[:, cols], 0), keys[cols], NN)
            peak = jnp.max(scores, axis=1, keepdims=True)
            expo = jnp.exp(scores - peak).astype(jnp.bfloat16)
            with_ones = jnp.where(rows // DH == number, values[cols], 1)
            results.append(dot(expo, with_ones, NT))
            total = results[-1] if number else pltpu.roll(results[-1], DH, 1)
            peaks = jnp.where(lanes == head, peak, peaks)
            totals = jnp.where(lanes == head, total, totals)
        part_out[:, cols] = jnp.where(lanes < DH, *results).astype(jnp.bfloat16)
    room = heads // 2
    stats = jnp.zeros((slots, STATS), jnp.float32)
    number = 0
    for value, terms in ((peaks, 3), (totals, 2)):
        for _ in range(terms):
            term = value.astype(jnp.bfloat16).astype(jnp.float32)
            value = value - term
            stats = stats + (pltpu.roll(term, number * room, 1) if number else term)
            number += 1
    part_out[:, half_width:] = stats.astype(jnp.bfloat16)


def merge_kernel(heads, parts, gain, packed_out):
    count, slots, _ = parts.shape
    half_width = packed_out.shape[2] // 2
    room = heads // 2
    stats = parts[:, :, half_width:].astype(jnp.float32).reshape(count * slots, STATS)

    def term(number):
        return pltpu.roll(stats, STATS - number * room, 1) if number else stats

    peaks = (term(0) + term(1) + term(2)).reshape(count // 2, 2, slots, STATS)
    totals = (term(3) + term(4)).reshape(count // 2, 2, slots, STATS)
    lanes = lax.broadcasted_iota(jnp.int32, peaks.shape, 3)
    peaks = jnp.where(lanes < room, peaks, 0.0)
    factors = jnp.exp(peaks - jnp.max(peaks, axis=0, keepdims=True))
    total = jnp.sum(factors * totals, axis=0)
    spread_rows = lax.broadcasted_iota(jnp.int32, (STATS, half_width), 0)
    spread_cols = lax.broadcasted_iota(jnp.int32, (STATS, half_width), 1)
    spread = ((spread_cols // DH) == spread_rows).astype(jnp.float32)

    def spread_out(value):
        return lax.dot_general(
            value, spread, NN, precision=lax.Precision.HIGHEST, preferred_element_type=jnp.float32
        )

    wide = spread_out(factors.reshape(count * slots, STATS)).reshape(
        count // 2, 2, slots, half_width
    )
    numer = parts[:, :, :half_width].astype(jnp.float32).reshape(wide.shape)
    numer = jnp.sum(wide * numer, axis=0)
    wide_total = spread_out(total.reshape(2 * slots, STATS)).reshape(2, slots, half_width)
    ratio = numer / wide_total
    raw = jnp.concatenate([ratio[0], ratio[1]], axis=1)
    centred = raw - jnp.mean(raw, axis=1, keepdims=True)
    variance = jnp.mean(centred * centred, axis=1, keepdims=True)
    packed = (centred * lax.rsqrt(variance + 1e-06) * gain[...]).astype(jnp.bfloat16)
    packed_out[...] = jnp.broadcast_to(packed[None], packed_out.shape)


def tail_kernel(heads, packed_a, packed_b, query_fwd, query_rev, pairing, seat, *refs):
    own, near, near_swapped, far, far_swapped, out, queries, weight, attended = refs
    width = queries.shape[1]
    length = out.shape[0]
    x, core = seat[3], seat[2]
    block = width // X
    half = weight.shape[0] // 2

    def columns(number):
        return pl.ds(pl.multiple_of(lax.rem(number + X, X) * block, block), block)

    weight[:, columns(x)] = own[...]
    weight[:, columns(x + 2 * core - 1)] = near[...]
    weight[:, columns(x + 1 - 2 * core)] = near_swapped[...]
    weight[pl.ds(pl.multiple_of(core * half, half), half), columns(x + 2)] = far[...]
    weight[pl.ds(pl.multiple_of((1 - core) * half, half), half), columns(x + 2)] = far_swapped[...]
    queries[:length] = query_fwd[...]
    queries[length:] = query_rev[...]
    packed = jnp.concatenate([packed_a[...], packed_b[...]], axis=0)
    keys = dot(weight[:width], packed, NT).astype(jnp.bfloat16)
    values = dot(packed, weight[width : 2 * width], NT).astype(jnp.bfloat16)
    lanes = lax.broadcasted_iota(jnp.int32, (2 * length, 2 * DH), 1)
    slot_lanes = lax.broadcasted_iota(jnp.int32, (values.shape[0], 2 * DH), 1)
    for pair in range(heads // 2):
        cols = slice(pair * 2 * DH, (pair + 1) * 2 * DH)
        query_pair = queries[:, cols] * SCALE
        results = []
        for number in range(2):
            scores = dot(jnp.where(lanes // DH == number, query_pair, 0), keys[cols], NN)
            expo = jnp.exp(scores - jnp.max(scores, axis=1, keepdims=True)).astype(jnp.bfloat16)
            with_ones = jnp.where(slot_lanes // DH == number, values[:, cols], 1)
            results.append(dot(expo, with_ones, NN))
        numer = jnp.where(lanes < DH, *results)
        total = pltpu.roll(jnp.where(lanes < DH, *results[::-1]), DH, 1)
        attended[:, cols] = (numer / total).astype(jnp.bfloat16)
    order = lax.broadcasted_iota(jnp.int32, (length, length), 0)
    order = order + lax.broadcasted_iota(jnp.int32, (length, length), 1) == length - 1
    flipped = dot(order.astype(jnp.bfloat16), attended[length:], NN).astype(jnp.bfloat16)
    attended[length:] = flipped
    mixed = dot(attended[...], weight[2 * width :], NT)
    reverse = mixed[length:]
    upper = reverse.astype(jnp.bfloat16)
    lower = (reverse - upper.astype(jnp.float32)).astype(jnp.bfloat16)
    paired = dot(upper, pairing[...], NN) + dot(lower, pairing[...], NN)
    out[...] = (mixed[:length] + paired).astype(jnp.bfloat16)


def params(mib):
    return pltpu.CompilerParams(vmem_limit_bytes=mib * MIB)


VMEM = pl.BlockSpec(memory_space=pltpu.VMEM)
SMEM = pl.BlockSpec(memory_space=pltpu.SMEM)


def shards(
    tokens,
    fwd_states,
    rev_states,
    conv_weight,
    embedding,
    in_weight,
    pack_query,
    pack_gain,
    tail_weight,
    channel_perm,
):
    local_len = tokens.shape[0]
    width = fwd_states.shape[1]
    slots = pack_query.shape[0]
    heads = width // DH
    count = lax.axis_size("seq")
    own_slots = slots // count
    place = lax.axis_index("seq")
    x = lax.axis_index("batch") // 2
    core = place % 2
    seat = jnp.stack([place // (2 * Z), place // 2 % Z, core, x]).astype(jnp.int32)

    block = width // X
    tail_block = lax.dynamic_slice_in_dim(tail_weight.T, x * block, block, 1)
    shard = jnp.concatenate([in_weight.T, tail_block], axis=1)
    across = send(shard, Y_OPPOSITE)
    held = [
        ((number,), jnp.stack([mine, send(mine, CORE_SWAP)]))
        for number, mine in enumerate((shard, across))
    ]
    pieces = [((halves, 0, False, False), piece) for halves, piece in held]
    x_own = strand_inputs(tokens, fwd_states, rev_states, conv_weight, embedding)
    pairing = (
        lax.broadcasted_iota(jnp.int32, (width, width), 0) == channel_perm[None, :]
    ).astype(jnp.bfloat16)
    rounds = 1 + (channel_perm[0] >> 31)
    x_own, pairing, rounds = lax.optimization_barrier((x_own, pairing, rounds))
    x_other = send(x_own, CORE_SWAP)
    for step in range(1, Z // 2 + 1):
        held, brought = ring_step(held, step, core)
        pieces += brought
    places, pieces = zip(*pieces)

    part, query_fwd, query_rev, own = pl.pallas_call(
        functools.partial(pack_kernel, places, heads),
        out_shape=(
            jax.ShapeDtypeStruct((slots, width // 2 + STATS), jnp.bfloat16),
            jax.ShapeDtypeStruct((local_len, width), jnp.bfloat16),
            jax.ShapeDtypeStruct((local_len, width), jnp.bfloat16),
            jax.ShapeDtypeStruct((3 * width, block), jnp.bfloat16),
        ),
        in_specs=[VMEM, VMEM, VMEM, SMEM] + [VMEM] * len(pieces),
        out_specs=(VMEM,) * 4,
        scratch_shapes=[
            pltpu.VMEM((3 * width, width), jnp.bfloat16),
            pltpu.VMEM((4 * local_len, width), jnp.bfloat16),
        ],
        compiler_params=params(20),
        name="pack",
    )(x_own, x_other, pack_query, seat, *pieces)

    near = send(own, X_RING)
    mirror = [(i, count - 1 - i) for i in range(count)]
    query_rev = lax.ppermute(query_rev, "seq", mirror)
    _, parts = lax.while_loop(
        lambda state: state[0] < rounds,
        lambda state: (state[0] + 1, lax.all_to_all(state[1], "seq", 0, 0)),
        (jnp.int32(0), part.reshape(count, own_slots, -1)),
    )
    parts, near, query_rev = lax.optimization_barrier((parts, near, query_rev))
    near_swapped = send(near, CORE_SWAP)
    half = 3 * width // 2
    far = send(lax.dynamic_slice_in_dim(near, core * half, half, 0), X_RING)
    copies = pl.pallas_call(
        functools.partial(merge_kernel, heads),
        out_shape=jax.ShapeDtypeStruct((count // 2, own_slots, width), jnp.bfloat16),
        in_specs=[VMEM, VMEM],
        out_specs=VMEM,
        compiler_params=params(12),
        name="merge",
    )(parts, pack_gain[None, :])

    same_core = [list(range(core, count, 2)) for core in range(2)]
    packed_a = lax.all_to_all(copies, "seq", 0, 0, axis_index_groups=same_core)
    packed_a = packed_a.reshape(slots // 2, width)
    packed_a, far, near_swapped = lax.optimization_barrier((packed_a, far, near_swapped))
    packed_b = send(packed_a, CORE_SWAP)
    far_swapped = send(far, CORE_SWAP)

    return pl.pallas_call(
        functools.partial(tail_kernel, heads),
        out_shape=jax.ShapeDtypeStruct((local_len, width), jnp.bfloat16),
        in_specs=[VMEM] * 5 + [SMEM] + [VMEM] * 5,
        out_specs=VMEM,
        scratch_shapes=[
            pltpu.VMEM((2 * local_len, width), jnp.bfloat16),
            pltpu.VMEM((3 * width, width), jnp.bfloat16),
            pltpu.VMEM((2 * local_len, width), jnp.bfloat16),
        ],
        compiler_params=params(20),
        name="tail",
    )(
        packed_a,
        packed_b,
        query_fwd,
        query_rev,
        pairing,
        seat,
        own,
        near,
        near_swapped,
        far,
        far_swapped,
    )


def solution(mesh):
    in_specs = (
        P(("batch", "seq")),
        P(("batch", "seq"), None),
        P(("batch", "seq"), None),
        P(),
        P(),
        P(None, "seq"),
        P(),
        P(),
        P(None, "seq"),
        P(),
    )
    out_specs = P(("batch", "seq"), None)
    return jax.shard_map(shards, mesh=mesh, in_specs=in_specs, out_specs=out_specs, check_vma=False)
```

```python
import functools
import math

import jax
import jax.numpy as jnp
from jax import lax
from jax.experimental import pallas as pl
from jax.experimental.pallas import tpu as pltpu
from jax.sharding import PartitionSpec as P

DH = 64
STATS = 128
LATE = 1
SCALE = 1.0 / math.sqrt(DH)
MIB = 1024 * 1024
NT = (((1,), (1,)), ((), ()))
NN = (((1,), (0,)), ((), ()))

Z, X = 8, 4
AXES = ("seq", "batch")


def device_index(x, y, z, core):
    y_hi, y_lo = divmod(y % 4, 2)
    return (y_hi * 2 * Z + (z % Z) * 2 + core) * 2 * X + (x % X) * 2 + y_lo


def moves(target):
    return [
        (device_index(x, y, z, core), device_index(*target(x, y, z, core)))
        for x in range(X)
        for y in range(4)
        for z in range(Z)
        for core in range(2)
    ]


RING = moves(lambda x, y, z, core: (x, y, z + 1 - 2 * core, core))
Y_OPPOSITE = moves(lambda x, y, z, core: (x, 3 - y, z, core))
X_RING = moves(lambda x, y, z, core: (x + 1 - 2 * core, y, z, core))
CORE_SWAP = moves(lambda x, y, z, core: (x, y, z, 1 - core))


def send(shard, pairs):
    return lax.ppermute(shard, AXES, pairs)


def dot(a, b, dims):
    return lax.dot_general(a, b, dims, preferred_element_type=jnp.float32)


def as_column(row, backwards):
    length = row.shape[1]
    down = lax.broadcasted_iota(jnp.int32, (length, length), 0)
    across = lax.broadcasted_iota(jnp.int32, (length, length), 1)
    wanted = down + across == length - 1 if backwards else down == across
    return jnp.sum(jnp.where(wanted, row, 0.0), axis=1, keepdims=True)


def inputs_kernel(fwd, rev, rims, symbols, taps, embedding, rows_out):
    length = fwd.shape[0]
    for strand, states in enumerate((fwd, rev)):
        rim = rims[strand].astype(jnp.float32)
        extended = jnp.concatenate([rim, states[...].astype(jnp.float32)], axis=0)
        total = jnp.zeros(states.shape, jnp.float32)
        for lag in range(taps.shape[0]):
            begin = rim.shape[0] - lag
            total = total + taps[lag : lag + 1] * extended[begin : begin + length]
        hidden = total.astype(jnp.bfloat16).astype(jnp.float32)
        ids = as_column(symbols[strand : strand + 1], strand == 1)
        if strand == 1:
            ids = jnp.where(ids == 4.0, 4.0, 3.0 - ids)
        added = jnp.zeros(states.shape, jnp.float32)
        for symbol in range(embedding.shape[0]):
            row = embedding[symbol : symbol + 1]
            added = added + jnp.where(ids == float(symbol), row, 0.0)
        rows_out[strand * length : (strand + 1) * length] = (hidden + added).astype(jnp.bfloat16)


def strand_edges(tokens, fwd_states, rev_states):
    keep = tokens.shape[0] - 8
    count = lax.axis_size("seq")
    rims = jnp.stack([fwd_states[keep:], rev_states[keep:]])
    rims = lax.ppermute(rims, "seq", [(i, i + 1) for i in range(count - 1)])
    opposite = lax.ppermute(tokens, "seq", [(i, count - 1 - i) for i in range(count)])
    return rims, opposite


def strand_inputs(tokens, fwd_states, rev_states, rims, opposite, conv_weight, embedding):
    local_len, width = fwd_states.shape
    symbols = jnp.stack([tokens, opposite]).astype(jnp.float32)
    return pl.pallas_call(
        inputs_kernel,
        out_shape=jax.ShapeDtypeStruct((2 * local_len, width), jnp.bfloat16),
        in_specs=[VMEM] * 6,
        out_specs=VMEM,
        compiler_params=params(16),
        name="inputs",
    )(fwd_states, rev_states, rims, symbols, conv_weight, embedding)


def ring_step(held, step, core):
    last = step == Z // 2
    moved = []
    for halves, piece in held:
        if last:
            half = piece.shape[1] // 2
            piece = lax.dynamic_slice_in_dim(piece, core * half, half, 1)
        moved.append((halves, send(piece, RING)))
    own = [((halves, step, False, last), piece) for halves, piece in moved]
    swapped = [((halves, step, True, last), send(piece, CORE_SWAP)) for halves, piece in moved]
    return moved, own + swapped


def put_in_order(places, piece_refs, seat, weight, tail_part):
    y_hi, z, core = seat[0], seat[1], seat[2]
    columns = weight.shape[0] // 32
    width = weight.shape[1]
    for (halves, step, swapped, halved), source in zip(places, piece_refs):
        rows = source.shape[1]
        ring = 1 - core if swapped else core
        from_z = lax.rem(z + (2 * ring - 1) * step + Z, Z)
        for number in range(source.shape[0]):
            from_y = 1 - y_hi if halves[number // 2] else y_hi
            from_core = 1 - ring if number % 2 else ring
            begin = (from_y * 2 * Z + from_z * 2 + from_core) * columns
            if halved:
                begin = begin + ring * rows
            into = pl.ds(pl.multiple_of(begin, 16), rows)
            weight[into] = source[number, :, :width]
            tail_part[into] = source[number, :, width:]


def pack_kernel(places, heads, x_own, x_other, query, seat, *refs):
    count = len(places)
    piece_refs = refs[:count]
    part_out, query_fwd, query_rev, tail_part, weight, inputs, late, pack_query, sems = refs[count:]
    fetches = [
        pltpu.make_async_copy(piece_refs[LATE], late, sems.at[0]),
        pltpu.make_async_copy(query, pack_query, sems.at[1]),
    ]
    for fetch in fetches:
        fetch.start()
    own_rows = x_own.shape[0]
    width = x_own.shape[1]
    half_width = width // 2
    core = seat[2]
    early = [number for number in range(count) if number != LATE]
    put_in_order(
        [places[number] for number in early],
        [piece_refs[number] for number in early],
        seat,
        weight,
        tail_part,
    )
    fetches[0].wait()
    put_in_order([places[LATE]], [late], seat, weight, tail_part)
    inputs[:own_rows] = x_own[...]
    inputs[own_rows:] = x_other[...]
    base = pl.multiple_of(core * half_width, half_width)
    rows_in = inputs[...]
    keys = dot(weight[pl.ds(base, half_width)], rows_in, NT).astype(jnp.bfloat16)
    values = dot(weight[pl.ds(base + width, half_width)], rows_in, NT).astype(jnp.bfloat16)
    queries = dot(x_own[...], weight[2 * width :], NT).astype(jnp.bfloat16)
    query_fwd[...] = queries[: own_rows // 2]
    query_rev[...] = queries[own_rows // 2 :]
    slots = query.shape[0]
    lanes = lax.broadcasted_iota(jnp.int32, (slots, STATS), 1)
    rows = lax.broadcasted_iota(jnp.int32, (2 * DH, inputs.shape[0]), 0)
    peaks = jnp.zeros((slots, STATS), jnp.float32)
    totals = jnp.zeros((slots, STATS), jnp.float32)
    fetches[1].wait()
    query_half = pack_query[:, pl.ds(base, half_width)] * SCALE
    for pair in range(heads // 4):
        cols = slice(pair * 2 * DH, (pair + 1) * 2 * DH)
        results = []
        for number in range(2):
            head = 2 * pair + number
            mine = lanes // DH == number
            scores = dot(jnp.where(mine, query_half[:, cols], 0), keys[cols], NN)
            peak = jnp.max(scores, axis=1, keepdims=True)
            expo = jnp.exp(scores - peak).astype(jnp.bfloat16)
            with_ones = jnp.where(rows // DH == number, values[cols], 1)
            results.append(dot(expo, with_ones, NT))
            total = results[-1] if number else pltpu.roll(results[-1], DH, 1)
            peaks = jnp.where(lanes == head, peak, peaks)
            totals = jnp.where(lanes == head, total, totals)
        part_out[:, cols] = jnp.where(lanes < DH, *results).astype(jnp.bfloat16)
    room = heads // 2
    stats = jnp.zeros((slots, STATS), jnp.float32)
    number = 0
    for value, terms in ((peaks, 3), (totals, 2)):
        for _ in range(terms):
            term = value.astype(jnp.bfloat16).astype(jnp.float32)
            value = value - term
            stats = stats + (pltpu.roll(term, number * room, 1) if number else term)
            number += 1
    part_out[:, half_width:] = stats.astype(jnp.bfloat16)


def merge_kernel(heads, parts, gain, packed_out):
    count, slots, _ = parts.shape
    half_width = packed_out.shape[2] // 2
    room = heads // 2
    stats = parts[:, :, half_width:].astype(jnp.float32).reshape(count * slots, STATS)

    def term(number):
        return pltpu.roll(stats, STATS - number * room, 1) if number else stats

    peaks = (term(0) + term(1) + term(2)).reshape(count // 2, 2, slots, STATS)
    totals = (term(3) + term(4)).reshape(count // 2, 2, slots, STATS)
    lanes = lax.broadcasted_iota(jnp.int32, peaks.shape, 3)
    peaks = jnp.where(lanes < room, peaks, 0.0)
    factors = jnp.exp(peaks - jnp.max(peaks, axis=0, keepdims=True))
    total = jnp.sum(factors * totals, axis=0)
    spread_rows = lax.broadcasted_iota(jnp.int32, (STATS, half_width), 0)
    spread_cols = lax.broadcasted_iota(jnp.int32, (STATS, half_width), 1)
    spread = ((spread_cols // DH) == spread_rows).astype(jnp.float32)

    def spread_out(value):
        return lax.dot_general(
            value, spread, NN, precision=lax.Precision.HIGHEST, preferred_element_type=jnp.float32
        )

    wide = spread_out(factors.reshape(count * slots, STATS)).reshape(
        count // 2, 2, slots, half_width
    )
    numer = parts[:, :, :half_width].astype(jnp.float32).reshape(wide.shape)
    numer = jnp.sum(wide * numer, axis=0)
    wide_total = spread_out(total.reshape(2 * slots, STATS)).reshape(2, slots, half_width)
    ratio = numer / wide_total
    raw = jnp.concatenate([ratio[0], ratio[1]], axis=1)
    centred = raw - jnp.mean(raw, axis=1, keepdims=True)
    variance = jnp.mean(centred * centred, axis=1, keepdims=True)
    packed = (centred * lax.rsqrt(variance + 1e-06) * gain[...]).astype(jnp.bfloat16)
    packed_out[...] = jnp.broadcast_to(packed[None], packed_out.shape)


def tail_kernel(heads, packed_a, packed_b, query_fwd, query_rev, pairing, seat, *refs):
    own, near, near_swapped, far, far_swapped, out, queries, weight, attended = refs
    width = queries.shape[1]
    length = out.shape[0]
    x, core = seat[3], seat[2]
    block = width // X
    half = weight.shape[0] // 2

    def columns(number):
        return pl.ds(pl.multiple_of(lax.rem(number + X, X) * block, block), block)

    weight[:, columns(x)] = own[...]
    weight[:, columns(x + 2 * core - 1)] = near[...]
    weight[:, columns(x + 1 - 2 * core)] = near_swapped[...]
    weight[pl.ds(pl.multiple_of(core * half, half), half), columns(x + 2)] = far[...]
    weight[pl.ds(pl.multiple_of((1 - core) * half, half), half), columns(x + 2)] = far_swapped[...]
    queries[:length] = query_fwd[...]
    queries[length:] = query_rev[...]
    packed = jnp.concatenate([packed_a[...], packed_b[...]], axis=0)
    keys = dot(weight[:width], packed, NT).astype(jnp.bfloat16)
    values = dot(packed, weight[width : 2 * width], NT).astype(jnp.bfloat16)
    lanes = lax.broadcasted_iota(jnp.int32, (2 * length, 2 * DH), 1)
    slot_lanes = lax.broadcasted_iota(jnp.int32, (values.shape[0], 2 * DH), 1)
    for pair in range(heads // 2):
        cols = slice(pair * 2 * DH, (pair + 1) * 2 * DH)
        query_pair = queries[:, cols] * SCALE
        results = []
        for number in range(2):
            scores = dot(jnp.where(lanes // DH == number, query_pair, 0), keys[cols], NN)
            expo = jnp.exp(scores - jnp.max(scores, axis=1, keepdims=True)).astype(jnp.bfloat16)
            with_ones = jnp.where(slot_lanes // DH == number, values[:, cols], 1)
            results.append(dot(expo, with_ones, NN))
        numer = jnp.where(lanes < DH, *results)
        total = pltpu.roll(jnp.where(lanes < DH, *results[::-1]), DH, 1)
        attended[:, cols] = (numer / total).astype(jnp.bfloat16)
    order = lax.broadcasted_iota(jnp.int32, (length, length), 0)
    order = order + lax.broadcasted_iota(jnp.int32, (length, length), 1) == length - 1
    flipped = dot(order.astype(jnp.bfloat16), attended[length:], NN).astype(jnp.bfloat16)
    attended[length:] = flipped
    mixed = dot(attended[...], weight[2 * width :], NT)
    reverse = mixed[length:]
    upper = reverse.astype(jnp.bfloat16)
    lower = (reverse - upper.astype(jnp.float32)).astype(jnp.bfloat16)
    paired = dot(upper, pairing[...], NN) + dot(lower, pairing[...], NN)
    out[...] = (mixed[:length] + paired).astype(jnp.bfloat16)


def params(mib):
    return pltpu.CompilerParams(vmem_limit_bytes=mib * MIB)


VMEM = pl.BlockSpec(memory_space=pltpu.VMEM)
HBM = pl.BlockSpec(memory_space=pltpu.HBM)
SMEM = pl.BlockSpec(memory_space=pltpu.SMEM)


def shards(
    tokens,
    fwd_states,
    rev_states,
    conv_weight,
    embedding,
    in_weight,
    pack_query,
    pack_gain,
    tail_weight,
    channel_perm,
):
    local_len = tokens.shape[0]
    width = fwd_states.shape[1]
    slots = pack_query.shape[0]
    heads = width // DH
    count = lax.axis_size("seq")
    own_slots = slots // count
    place = lax.axis_index("seq")
    x = lax.axis_index("batch") // 2
    core = place % 2
    seat = jnp.stack([place // (2 * Z), place // 2 % Z, core, x]).astype(jnp.int32)

    block = width // X
    tail_block = lax.dynamic_slice_in_dim(tail_weight.T, x * block, block, 1)
    shard = jnp.concatenate([in_weight.T, tail_block], axis=1)
    across = send(shard, Y_OPPOSITE)
    rims, opposite = strand_edges(tokens, fwd_states, rev_states)
    across, rims = lax.optimization_barrier((across, rims))
    held = [
        ((number,), jnp.stack([mine, send(mine, CORE_SWAP)]))
        for number, mine in enumerate((shard, across))
    ]
    pieces = [((halves, 0, False, False), piece) for halves, piece in held]
    pairing = (
        lax.broadcasted_iota(jnp.int32, (width, width), 0) == channel_perm[None, :]
    ).astype(jnp.bfloat16)
    x_own = strand_inputs(
        tokens, fwd_states, rev_states, rims, opposite, conv_weight, embedding
    )
    x_own, pairing = lax.optimization_barrier((x_own, pairing))
    x_other = send(x_own, CORE_SWAP)
    for step in range(1, Z // 2 + 1):
        held, brought = ring_step(held, step, core)
        pieces += brought
    places, pieces = zip(*pieces)

    fetched = pltpu.with_memory_space_constraint(pieces[LATE], pltpu.HBM)
    pieces = [*pieces[:LATE], fetched, *pieces[LATE + 1 :]]
    part, query_fwd, query_rev, own = pl.pallas_call(
        functools.partial(pack_kernel, places, heads),
        out_shape=(
            jax.ShapeDtypeStruct((slots, width // 2 + STATS), jnp.bfloat16),
            jax.ShapeDtypeStruct((local_len, width), jnp.bfloat16),
            jax.ShapeDtypeStruct((local_len, width), jnp.bfloat16),
            jax.ShapeDtypeStruct((3 * width, block), jnp.bfloat16),
        ),
        in_specs=[VMEM, VMEM, HBM, SMEM, VMEM, HBM] + [VMEM] * (len(pieces) - 2),
        out_specs=(VMEM,) * 4,
        scratch_shapes=[
            pltpu.VMEM((3 * width, width), jnp.bfloat16),
            pltpu.VMEM((4 * local_len, width), jnp.bfloat16),
            pltpu.VMEM(pieces[LATE].shape, jnp.bfloat16),
            pltpu.VMEM((slots, width), jnp.bfloat16),
            pltpu.SemaphoreType.DMA((2,)),
        ],
        compiler_params=params(20),
        name="pack",
    )(
        x_own,
        x_other,
        pltpu.with_memory_space_constraint(pack_query, pltpu.HBM),
        seat,
        *pieces,
    )

    near = send(own, X_RING)
    mirror = [(i, count - 1 - i) for i in range(count)]
    query_rev = lax.ppermute(query_rev, "seq", mirror)
    rounds = 1 + (place >> 31)
    _, parts = lax.while_loop(
        lambda state: state[0] < rounds,
        lambda state: (state[0] + 1, lax.all_to_all(state[1], "seq", 0, 0)),
        (jnp.int32(0), part.reshape(count, own_slots, -1)),
    )
    parts, near, query_rev = lax.optimization_barrier((parts, near, query_rev))
    near_swapped = send(near, CORE_SWAP)
    half = 3 * width // 2
    far = send(lax.dynamic_slice_in_dim(near, core * half, half, 0), X_RING)
    copies = pl.pallas_call(
        functools.partial(merge_kernel, heads),
        out_shape=jax.ShapeDtypeStruct((count // 2, own_slots, width), jnp.bfloat16),
        in_specs=[VMEM, VMEM],
        out_specs=VMEM,
        compiler_params=params(12),
        name="merge",
    )(parts, pack_gain[None, :])

    same_core = [list(range(core, count, 2)) for core in range(2)]
    packed_a = lax.all_to_all(copies, "seq", 0, 0, axis_index_groups=same_core)
    packed_a = packed_a.reshape(slots // 2, width)
    packed_a, far, near_swapped = lax.optimization_barrier((packed_a, far, near_swapped))
    packed_b = send(packed_a, CORE_SWAP)
    far_swapped = send(far, CORE_SWAP)

    return pl.pallas_call(
        functools.partial(tail_kernel, heads),
        out_shape=jax.ShapeDtypeStruct((local_len, width), jnp.bfloat16),
        in_specs=[VMEM] * 5 + [SMEM] + [VMEM] * 5,
        out_specs=VMEM,
        scratch_shapes=[
            pltpu.VMEM((2 * local_len, width), jnp.bfloat16),
            pltpu.VMEM((3 * width, width), jnp.bfloat16),
            pltpu.VMEM((2 * local_len, width), jnp.bfloat16),
        ],
        compiler_params=params(20),
        name="tail",
    )(
        packed_a,
        packed_b,
        query_fwd,
        query_rev,
        pairing,
        seat,
        own,
        near,
        near_swapped,
        far,
        far_swapped,
    )


def solution(mesh):
    in_specs = (
        P(("batch", "seq")),
        P(("batch", "seq"), None),
        P(("batch", "seq"), None),
        P(),
        P(),
        P(None, "seq"),
        P(),
        P(),
        P(None, "seq"),
        P(),
    )
    out_specs = P(("batch", "seq"), None)
    return jax.shard_map(shards, mesh=mesh, in_specs=in_specs, out_specs=out_specs, check_vma=False)
```

```python
import functools
import math

import jax
import jax.numpy as jnp
from jax import lax
from jax.experimental import pallas as pl
from jax.experimental.pallas import tpu as pltpu
from jax.sharding import PartitionSpec as P

DH = 64
STATS = 128
LATE = 1
SCALE = 1.0 / math.sqrt(DH)
MIB = 1024 * 1024
NT = (((1,), (1,)), ((), ()))
NN = (((1,), (0,)), ((), ()))

Z, X = 8, 4
AXES = ("seq", "batch")


def device_index(x, y, z, core):
    y_hi, y_lo = divmod(y % 4, 2)
    return (y_hi * 2 * Z + (z % Z) * 2 + core) * 2 * X + (x % X) * 2 + y_lo


def moves(target):
    return [
        (device_index(x, y, z, core), device_index(*target(x, y, z, core)))
        for x in range(X)
        for y in range(4)
        for z in range(Z)
        for core in range(2)
    ]


RING = moves(lambda x, y, z, core: (x, y, z + 1 - 2 * core, core))
Y_OPPOSITE = moves(lambda x, y, z, core: (x, 3 - y, z, core))
X_RING = moves(lambda x, y, z, core: (x + 1 - 2 * core, y, z, core))
CORE_SWAP = moves(lambda x, y, z, core: (x, y, z, 1 - core))


def send(shard, pairs):
    return lax.ppermute(shard, AXES, pairs)


def dot(a, b, dims):
    return lax.dot_general(a, b, dims, preferred_element_type=jnp.float32)


def as_column(row, backwards):
    length = row.shape[1]
    down = lax.broadcasted_iota(jnp.int32, (length, length), 0)
    across = lax.broadcasted_iota(jnp.int32, (length, length), 1)
    wanted = down + across == length - 1 if backwards else down == across
    return jnp.sum(jnp.where(wanted, row, 0.0), axis=1, keepdims=True)


def inputs_kernel(fwd, rev, rims, symbols, taps, embedding, rows_out):
    length = fwd.shape[0]
    for strand, states in enumerate((fwd, rev)):
        rim = rims[strand].astype(jnp.float32)
        extended = jnp.concatenate([rim, states[...].astype(jnp.float32)], axis=0)
        total = jnp.zeros(states.shape, jnp.float32)
        for lag in range(taps.shape[0]):
            begin = rim.shape[0] - lag
            total = total + taps[lag : lag + 1] * extended[begin : begin + length]
        hidden = total.astype(jnp.bfloat16).astype(jnp.float32)
        ids = as_column(symbols[strand : strand + 1], strand == 1)
        if strand == 1:
            ids = jnp.where(ids == 4.0, 4.0, 3.0 - ids)
        added = jnp.zeros(states.shape, jnp.float32)
        for symbol in range(embedding.shape[0]):
            row = embedding[symbol : symbol + 1]
            added = added + jnp.where(ids == float(symbol), row, 0.0)
        rows_out[strand * length : (strand + 1) * length] = (hidden + added).astype(jnp.bfloat16)


def strand_edges(tokens, fwd_states, rev_states):
    keep = tokens.shape[0] - 8
    count = lax.axis_size("seq")
    rims = jnp.stack([fwd_states[keep:], rev_states[keep:]])
    rims = lax.ppermute(rims, "seq", [(i, i + 1) for i in range(count - 1)])
    opposite = lax.ppermute(tokens, "seq", [(i, count - 1 - i) for i in range(count)])
    return rims, opposite


def strand_inputs(tokens, fwd_states, rev_states, rims, opposite, conv_weight, embedding):
    local_len, width = fwd_states.shape
    symbols = jnp.stack([tokens, opposite]).astype(jnp.float32)
    return pl.pallas_call(
        inputs_kernel,
        out_shape=jax.ShapeDtypeStruct((2 * local_len, width), jnp.bfloat16),
        in_specs=[VMEM] * 6,
        out_specs=VMEM,
        compiler_params=params(16),
        name="inputs",
    )(fwd_states, rev_states, rims, symbols, conv_weight, embedding)


def ring_step(held, step, core):
    last = step == Z // 2
    moved = []
    for halves, piece in held:
        if last:
            half = piece.shape[1] // 2
            piece = lax.dynamic_slice_in_dim(piece, core * half, half, 1)
        moved.append((halves, send(piece, RING)))
    own = [((halves, step, False, last), piece) for halves, piece in moved]
    swapped = [((halves, step, True, last), send(piece, CORE_SWAP)) for halves, piece in moved]
    return moved, own + swapped


def put_in_order(places, piece_refs, seat, weight, tail_part):
    y_hi, z, core = seat[0], seat[1], seat[2]
    columns = weight.shape[0] // 32
    width = weight.shape[1]
    for (halves, step, swapped, halved), source in zip(places, piece_refs):
        rows = source.shape[1]
        ring = 1 - core if swapped else core
        from_z = lax.rem(z + (2 * ring - 1) * step + Z, Z)
        for number in range(source.shape[0]):
            from_y = 1 - y_hi if halves[number // 2] else y_hi
            from_core = 1 - ring if number % 2 else ring
            begin = (from_y * 2 * Z + from_z * 2 + from_core) * columns
            if halved:
                begin = begin + ring * rows
            into = pl.ds(pl.multiple_of(begin, 16), rows)
            weight[into] = source[number, :, :width]
            tail_part[into] = source[number, :, width:]


def pack_kernel(places, heads, x_own, x_other, query, seat, *refs):
    count = len(places)
    piece_refs = refs[:count]
    part_out, query_fwd, query_rev, tail_part, weight, inputs, late, pack_query, sems = refs[count:]
    fetches = [
        pltpu.make_async_copy(piece_refs[LATE], late, sems.at[0]),
        pltpu.make_async_copy(query, pack_query, sems.at[1]),
    ]
    for fetch in fetches:
        fetch.start()
    own_rows = x_own.shape[0]
    width = x_own.shape[1]
    half_width = width // 2
    core = seat[2]
    early = [number for number in range(count) if number != LATE]
    put_in_order(
        [places[number] for number in early],
        [piece_refs[number] for number in early],
        seat,
        weight,
        tail_part,
    )
    fetches[0].wait()
    put_in_order([places[LATE]], [late], seat, weight, tail_part)
    inputs[:own_rows] = x_own[...]
    inputs[own_rows:] = x_other[...]
    base = pl.multiple_of(core * half_width, half_width)
    rows_in = inputs[...]
    keys = dot(weight[pl.ds(base, half_width)], rows_in, NT).astype(jnp.bfloat16)
    values = dot(weight[pl.ds(base + width, half_width)], rows_in, NT).astype(jnp.bfloat16)
    queries = dot(x_own[...], weight[2 * width :], NT).astype(jnp.bfloat16)
    query_fwd[...] = queries[: own_rows // 2]
    query_rev[...] = queries[own_rows // 2 :]
    slots = query.shape[0]
    lanes = lax.broadcasted_iota(jnp.int32, (slots, STATS), 1)
    rows = lax.broadcasted_iota(jnp.int32, (2 * DH, inputs.shape[0]), 0)
    peaks = jnp.zeros((slots, STATS), jnp.float32)
    totals = jnp.zeros((slots, STATS), jnp.float32)
    fetches[1].wait()
    query_half = pack_query[:, pl.ds(base, half_width)] * SCALE
    for pair in range(heads // 4):
        cols = slice(pair * 2 * DH, (pair + 1) * 2 * DH)
        results = []
        for number in range(2):
            head = 2 * pair + number
            mine = lanes // DH == number
            scores = dot(jnp.where(mine, query_half[:, cols], 0), keys[cols], NN)
            peak = jnp.max(scores, axis=1, keepdims=True)
            expo = jnp.exp(scores - peak).astype(jnp.bfloat16)
            with_ones = jnp.where(rows // DH == number, values[cols], 1)
            results.append(dot(expo, with_ones, NT))
            total = results[-1] if number else pltpu.roll(results[-1], DH, 1)
            peaks = jnp.where(lanes == head, peak, peaks)
            totals = jnp.where(lanes == head, total, totals)
        part_out[:, cols] = jnp.where(lanes < DH, *results).astype(jnp.bfloat16)
    room = heads // 2
    stats = jnp.zeros((slots, STATS), jnp.float32)
    number = 0
    for value, terms in ((peaks, 3), (totals, 2)):
        for _ in range(terms):
            term = value.astype(jnp.bfloat16).astype(jnp.float32)
            value = value - term
            stats = stats + (pltpu.roll(term, number * room, 1) if number else term)
            number += 1
    part_out[:, half_width:] = stats.astype(jnp.bfloat16)


def merge_kernel(heads, parts, gain, packed_out):
    count, slots, _ = parts.shape
    half_width = packed_out.shape[2] // 2
    room = heads // 2
    stats = parts[:, :, half_width:].astype(jnp.float32).reshape(count * slots, STATS)

    def term(number):
        return pltpu.roll(stats, STATS - number * room, 1) if number else stats

    peaks = (term(0) + term(1) + term(2)).reshape(count // 2, 2, slots, STATS)
    totals = (term(3) + term(4)).reshape(count // 2, 2, slots, STATS)
    lanes = lax.broadcasted_iota(jnp.int32, peaks.shape, 3)
    peaks = jnp.where(lanes < room, peaks, 0.0)
    factors = jnp.exp(peaks - jnp.max(peaks, axis=0, keepdims=True))
    total = jnp.sum(factors * totals, axis=0)
    spread_rows = lax.broadcasted_iota(jnp.int32, (STATS, half_width), 0)
    spread_cols = lax.broadcasted_iota(jnp.int32, (STATS, half_width), 1)
    spread = ((spread_cols // DH) == spread_rows).astype(jnp.float32)

    def spread_out(value):
        return lax.dot_general(
            value, spread, NN, precision=lax.Precision.HIGHEST, preferred_element_type=jnp.float32
        )

    wide = spread_out(factors.reshape(count * slots, STATS)).reshape(
        count // 2, 2, slots, half_width
    )
    numer = parts[:, :, :half_width].astype(jnp.float32).reshape(wide.shape)
    numer = jnp.sum(wide * numer, axis=0)
    wide_total = spread_out(total.reshape(2 * slots, STATS)).reshape(2, slots, half_width)
    ratio = numer / wide_total
    raw = jnp.concatenate([ratio[0], ratio[1]], axis=1)
    centred = raw - jnp.mean(raw, axis=1, keepdims=True)
    variance = jnp.mean(centred * centred, axis=1, keepdims=True)
    packed = (centred * lax.rsqrt(variance + 1e-06) * gain[...]).astype(jnp.bfloat16)
    packed_out[...] = jnp.broadcast_to(packed[None], packed_out.shape)


def tail_kernel(heads, packed_a, packed_b, query_fwd, query_rev, pairing, seat, *refs):
    own, near, near_swapped, far, far_swapped, out, queries, weight, attended = refs
    width = queries.shape[1]
    length = out.shape[0]
    x, core = seat[3], seat[2]
    block = width // X
    half = weight.shape[0] // 2

    def columns(number):
        return pl.ds(pl.multiple_of(lax.rem(number + X, X) * block, block), block)

    weight[:, columns(x)] = own[...]
    weight[:, columns(x + 2 * core - 1)] = near[...]
    weight[:, columns(x + 1 - 2 * core)] = near_swapped[...]
    weight[pl.ds(pl.multiple_of(core * half, half), half), columns(x + 2)] = far[...]
    weight[pl.ds(pl.multiple_of((1 - core) * half, half), half), columns(x + 2)] = far_swapped[...]
    queries[:length] = query_fwd[...]
    queries[length:] = query_rev[...]
    packed = jnp.concatenate([packed_a[...], packed_b[...]], axis=0)
    keys = dot(weight[:width], packed, NT).astype(jnp.bfloat16)
    values = dot(packed, weight[width : 2 * width], NT).astype(jnp.bfloat16)
    lanes = lax.broadcasted_iota(jnp.int32, (2 * length, 2 * DH), 1)
    slot_lanes = lax.broadcasted_iota(jnp.int32, (values.shape[0], 2 * DH), 1)
    for pair in range(heads // 2):
        cols = slice(pair * 2 * DH, (pair + 1) * 2 * DH)
        query_pair = queries[:, cols] * SCALE
        results = []
        for number in range(2):
            scores = dot(jnp.where(lanes // DH == number, query_pair, 0), keys[cols], NN)
            expo = jnp.exp(scores - jnp.max(scores, axis=1, keepdims=True)).astype(jnp.bfloat16)
            with_ones = jnp.where(slot_lanes // DH == number, values[:, cols], 1)
            results.append(dot(expo, with_ones, NN))
        numer = jnp.where(lanes < DH, *results)
        total = pltpu.roll(jnp.where(lanes < DH, *results[::-1]), DH, 1)
        attended[:, cols] = (numer / total).astype(jnp.bfloat16)
    order = lax.broadcasted_iota(jnp.int32, (length, length), 0)
    order = order + lax.broadcasted_iota(jnp.int32, (length, length), 1) == length - 1
    flipped = dot(order.astype(jnp.bfloat16), attended[length:], NN).astype(jnp.bfloat16)
    attended[length:] = flipped
    mixed = dot(attended[...], weight[2 * width :], NT)
    reverse = mixed[length:]
    upper = reverse.astype(jnp.bfloat16)
    lower = (reverse - upper.astype(jnp.float32)).astype(jnp.bfloat16)
    paired = dot(upper, pairing[...], NN) + dot(lower, pairing[...], NN)
    out[...] = (mixed[:length] + paired).astype(jnp.bfloat16)


def params(mib):
    return pltpu.CompilerParams(vmem_limit_bytes=mib * MIB)


VMEM = pl.BlockSpec(memory_space=pltpu.VMEM)
HBM = pl.BlockSpec(memory_space=pltpu.HBM)
SMEM = pl.BlockSpec(memory_space=pltpu.SMEM)


def shards(
    tokens,
    fwd_states,
    rev_states,
    conv_weight,
    embedding,
    in_weight,
    pack_query,
    pack_gain,
    tail_weight,
    channel_perm,
):
    local_len = tokens.shape[0]
    width = fwd_states.shape[1]
    slots = pack_query.shape[0]
    heads = width // DH
    count = lax.axis_size("seq")
    own_slots = slots // count
    place = lax.axis_index("seq")
    x = lax.axis_index("batch") // 2
    core = place % 2
    seat = jnp.stack([place // (2 * Z), place // 2 % Z, core, x]).astype(jnp.int32)

    block = width // X
    tail_block = lax.dynamic_slice_in_dim(tail_weight.T, x * block, block, 1)
    shard = jnp.concatenate([in_weight.T, tail_block], axis=1)
    across = send(shard, Y_OPPOSITE)
    rims, opposite = strand_edges(tokens, fwd_states, rev_states)
    across, rims = lax.optimization_barrier((across, rims))
    held = [
        ((number,), jnp.stack([mine, send(mine, CORE_SWAP)]))
        for number, mine in enumerate((shard, across))
    ]
    pieces = [((halves, 0, False, False), piece) for halves, piece in held]
    pairing = (
        lax.broadcasted_iota(jnp.int32, (width, width), 0) == channel_perm[None, :]
    ).astype(jnp.bfloat16)
    x_own = strand_inputs(
        tokens, fwd_states, rev_states, rims, opposite, conv_weight, embedding
    )
    x_own, pairing = lax.optimization_barrier((x_own, pairing))
    x_other = send(x_own, CORE_SWAP)
    for step in range(1, Z // 2 + 1):
        held, brought = ring_step(held, step, core)
        pieces += brought
    places, pieces = zip(*pieces)

    fetched = pltpu.with_memory_space_constraint(pieces[LATE], pltpu.HBM)
    pieces = [*pieces[:LATE], fetched, *pieces[LATE + 1 :]]
    part, query_fwd, query_rev, own = pl.pallas_call(
        functools.partial(pack_kernel, places, heads),
        out_shape=(
            jax.ShapeDtypeStruct((slots, width // 2 + STATS), jnp.bfloat16),
            jax.ShapeDtypeStruct((local_len, width), jnp.bfloat16),
            jax.ShapeDtypeStruct((local_len, width), jnp.bfloat16),
            jax.ShapeDtypeStruct((3 * width, block), jnp.bfloat16),
        ),
        in_specs=[VMEM, VMEM, HBM, SMEM, VMEM, HBM] + [VMEM] * (len(pieces) - 2),
        out_specs=(VMEM,) * 4,
        scratch_shapes=[
            pltpu.VMEM((3 * width, width), jnp.bfloat16),
            pltpu.VMEM((4 * local_len, width), jnp.bfloat16),
            pltpu.VMEM(pieces[LATE].shape, jnp.bfloat16),
            pltpu.VMEM((slots, width), jnp.bfloat16),
            pltpu.SemaphoreType.DMA((2,)),
        ],
        compiler_params=params(20),
        name="pack",
    )(
        x_own,
        x_other,
        pltpu.with_memory_space_constraint(pack_query, pltpu.HBM),
        seat,
        *pieces,
    )

    near = send(own, X_RING)
    mirror = [(i, count - 1 - i) for i in range(count)]
    query_rev = lax.ppermute(query_rev, "seq", mirror)
    parts = lax.cond(
        place >= 0,
        lambda rows: lax.all_to_all(rows, "seq", 0, 0),
        lambda rows: rows,
        part.reshape(count, own_slots, -1),
    )
    parts, near, query_rev = lax.optimization_barrier((parts, near, query_rev))
    near_swapped = send(near, CORE_SWAP)
    half = 3 * width // 2
    far = send(lax.dynamic_slice_in_dim(near, core * half, half, 0), X_RING)
    copies = pl.pallas_call(
        functools.partial(merge_kernel, heads),
        out_shape=jax.ShapeDtypeStruct((count // 2, own_slots, width), jnp.bfloat16),
        in_specs=[VMEM, VMEM],
        out_specs=VMEM,
        compiler_params=params(12),
        name="merge",
    )(parts, pack_gain[None, :])

    same_core = [list(range(core, count, 2)) for core in range(2)]
    packed_a = lax.all_to_all(copies, "seq", 0, 0, axis_index_groups=same_core)
    packed_a = packed_a.reshape(slots // 2, width)
    packed_a, far, near_swapped = lax.optimization_barrier((packed_a, far, near_swapped))
    packed_b = send(packed_a, CORE_SWAP)
    far_swapped = send(far, CORE_SWAP)

    return pl.pallas_call(
        functools.partial(tail_kernel, heads),
        out_shape=jax.ShapeDtypeStruct((local_len, width), jnp.bfloat16),
        in_specs=[VMEM] * 5 + [SMEM] + [VMEM] * 5,
        out_specs=VMEM,
        scratch_shapes=[
            pltpu.VMEM((2 * local_len, width), jnp.bfloat16),
            pltpu.VMEM((3 * width, width), jnp.bfloat16),
            pltpu.VMEM((2 * local_len, width), jnp.bfloat16),
        ],
        compiler_params=params(20),
        name="tail",
    )(
        packed_a,
        packed_b,
        query_fwd,
        query_rev,
        pairing,
        seat,
        own,
        near,
        near_swapped,
        far,
        far_swapped,
    )


def solution(mesh):
    in_specs = (
        P(("batch", "seq")),
        P(("batch", "seq"), None),
        P(("batch", "seq"), None),
        P(),
        P(),
        P(None, "seq"),
        P(),
        P(),
        P(None, "seq"),
        P(),
    )
    out_specs = P(("batch", "seq"), None)
    return jax.shard_map(shards, mesh=mesh, in_specs=in_specs, out_specs=out_specs, check_vma=False)
```

```python
import functools
import math

import jax
import jax.numpy as jnp
from jax import lax
from jax.experimental import pallas as pl
from jax.experimental.pallas import tpu as pltpu
from jax.sharding import PartitionSpec as P

DH = 64
STATS = 128
LATE = 1
SCALE = 1.0 / math.sqrt(DH)
MIB = 1024 * 1024
NT = (((1,), (1,)), ((), ()))
NN = (((1,), (0,)), ((), ()))

Z, X = 8, 4
AXES = ("seq", "batch")


def device_index(x, y, z, core):
    y_hi, y_lo = divmod(y % 4, 2)
    return (y_hi * 2 * Z + (z % Z) * 2 + core) * 2 * X + (x % X) * 2 + y_lo


def moves(target):
    return [
        (device_index(x, y, z, core), device_index(*target(x, y, z, core)))
        for x in range(X)
        for y in range(4)
        for z in range(Z)
        for core in range(2)
    ]


RING = moves(lambda x, y, z, core: (x, y, z + 1 - 2 * core, core))
Y_OPPOSITE = moves(lambda x, y, z, core: (x, 3 - y, z, core))
X_RING = moves(lambda x, y, z, core: (x + 1 - 2 * core, y, z, core))
CORE_SWAP = moves(lambda x, y, z, core: (x, y, z, 1 - core))


def send(shard, pairs):
    return lax.ppermute(shard, AXES, pairs)


def dot(a, b, dims):
    return lax.dot_general(a, b, dims, preferred_element_type=jnp.float32)


def as_column(row, backwards):
    length = row.shape[1]
    down = lax.broadcasted_iota(jnp.int32, (length, length), 0)
    across = lax.broadcasted_iota(jnp.int32, (length, length), 1)
    wanted = down + across == length - 1 if backwards else down == across
    return jnp.sum(jnp.where(wanted, row, 0.0), axis=1, keepdims=True)


def inputs_kernel(fwd, rev, rims, symbols, taps, embedding, rows_out):
    length = fwd.shape[0]
    for strand, states in enumerate((fwd, rev)):
        rim = rims[strand].astype(jnp.float32)
        extended = jnp.concatenate([rim, states[...].astype(jnp.float32)], axis=0)
        total = jnp.zeros(states.shape, jnp.float32)
        for lag in range(taps.shape[0]):
            begin = rim.shape[0] - lag
            total = total + taps[lag : lag + 1] * extended[begin : begin + length]
        hidden = total.astype(jnp.bfloat16).astype(jnp.float32)
        ids = as_column(symbols[strand : strand + 1], strand == 1)
        if strand == 1:
            ids = jnp.where(ids == 4.0, 4.0, 3.0 - ids)
        added = jnp.zeros(states.shape, jnp.float32)
        for symbol in range(embedding.shape[0]):
            row = embedding[symbol : symbol + 1]
            added = added + jnp.where(ids == float(symbol), row, 0.0)
        rows_out[strand * length : (strand + 1) * length] = (hidden + added).astype(jnp.bfloat16)


def strand_edges(tokens, fwd_states, rev_states):
    keep = tokens.shape[0] - 8
    count = lax.axis_size("seq")
    rims = jnp.stack([fwd_states[keep:], rev_states[keep:]])
    rims = lax.ppermute(rims, "seq", [(i, i + 1) for i in range(count - 1)])
    opposite = lax.ppermute(tokens, "seq", [(i, count - 1 - i) for i in range(count)])
    return rims, opposite


def strand_inputs(tokens, fwd_states, rev_states, rims, opposite, conv_weight, embedding):
    local_len, width = fwd_states.shape
    symbols = jnp.stack([tokens, opposite]).astype(jnp.float32)
    return pl.pallas_call(
        inputs_kernel,
        out_shape=jax.ShapeDtypeStruct((2 * local_len, width), jnp.bfloat16),
        in_specs=[VMEM] * 6,
        out_specs=VMEM,
        compiler_params=params(16),
        name="inputs",
    )(fwd_states, rev_states, rims, symbols, conv_weight, embedding)


def ring_step(held, step, core):
    last = step == Z // 2
    moved = []
    for halves, piece in held:
        if last:
            half = piece.shape[1] // 2
            piece = lax.dynamic_slice_in_dim(piece, core * half, half, 1)
        moved.append((halves, send(piece, RING)))
    own = [((halves, step, False, last), piece) for halves, piece in moved]
    swapped = [((halves, step, True, last), send(piece, CORE_SWAP)) for halves, piece in moved]
    return moved, own + swapped


def put_in_order(places, piece_refs, seat, weight, tail_part):
    y_hi, z, core = seat[0], seat[1], seat[2]
    columns = weight.shape[0] // 32
    width = weight.shape[1]
    for (halves, step, swapped, halved), source in zip(places, piece_refs):
        rows = source.shape[1]
        ring = 1 - core if swapped else core
        from_z = lax.rem(z + (2 * ring - 1) * step + Z, Z)
        for number in range(source.shape[0]):
            from_y = 1 - y_hi if halves[number // 2] else y_hi
            from_core = 1 - ring if number % 2 else ring
            begin = (from_y * 2 * Z + from_z * 2 + from_core) * columns
            if halved:
                begin = begin + ring * rows
            into = pl.ds(pl.multiple_of(begin, 16), rows)
            weight[into] = source[number, :, :width]
            tail_part[into] = source[number, :, width:]


def pack_kernel(places, heads, x_own, x_other, query, seat, *refs):
    count = len(places)
    piece_refs = refs[:count]
    part_out, query_fwd, query_rev, tail_part, weight, inputs, late, pack_query, sems = refs[count:]
    fetches = [
        pltpu.make_async_copy(piece_refs[LATE], late, sems.at[0]),
        pltpu.make_async_copy(query, pack_query, sems.at[1]),
    ]
    for fetch in fetches:
        fetch.start()
    own_rows = x_own.shape[0]
    width = x_own.shape[1]
    half_width = width // 2
    core = seat[2]
    early = [number for number in range(count) if number != LATE]
    put_in_order(
        [places[number] for number in early],
        [piece_refs[number] for number in early],
        seat,
        weight,
        tail_part,
    )
    inputs[:own_rows] = x_own[...]
    inputs[own_rows:] = x_other[...]
    fetches[0].wait()
    put_in_order([places[LATE]], [late], seat, weight, tail_part)
    base = pl.multiple_of(core * half_width, half_width)
    rows_in = inputs[...]
    keys = dot(weight[pl.ds(base, half_width)], rows_in, NT).astype(jnp.bfloat16)
    values = dot(weight[pl.ds(base + width, half_width)], rows_in, NT).astype(jnp.bfloat16)
    queries = dot(x_own[...], weight[2 * width :], NT).astype(jnp.bfloat16)
    query_fwd[...] = queries[: own_rows // 2]
    query_rev[...] = queries[own_rows // 2 :]
    slots = query.shape[0]
    lanes = lax.broadcasted_iota(jnp.int32, (slots, STATS), 1)
    rows = lax.broadcasted_iota(jnp.int32, (2 * DH, inputs.shape[0]), 0)
    peaks = jnp.zeros((slots, STATS), jnp.float32)
    totals = jnp.zeros((slots, STATS), jnp.float32)
    fetches[1].wait()
    query_half = pack_query[:, pl.ds(base, half_width)] * SCALE
    for pair in range(heads // 4):
        cols = slice(pair * 2 * DH, (pair + 1) * 2 * DH)
        results = []
        for number in range(2):
            head = 2 * pair + number
            mine = lanes // DH == number
            scores = dot(jnp.where(mine, query_half[:, cols], 0), keys[cols], NN)
            peak = jnp.max(scores, axis=1, keepdims=True)
            expo = jnp.exp(scores - peak).astype(jnp.bfloat16)
            with_ones = jnp.where(rows // DH == number, values[cols], 1)
            results.append(dot(expo, with_ones, NT))
            total = results[-1] if number else pltpu.roll(results[-1], DH, 1)
            peaks = jnp.where(lanes == head, peak, peaks)
            totals = jnp.where(lanes == head, total, totals)
        part_out[:, cols] = jnp.where(lanes < DH, *results).astype(jnp.bfloat16)
    room = heads // 2
    stats = jnp.zeros((slots, STATS), jnp.float32)
    number = 0
    for value, terms in ((peaks, 3), (totals, 2)):
        for _ in range(terms):
            term = value.astype(jnp.bfloat16).astype(jnp.float32)
            value = value - term
            stats = stats + (pltpu.roll(term, number * room, 1) if number else term)
            number += 1
    part_out[:, half_width:] = stats.astype(jnp.bfloat16)


def merge_kernel(heads, parts, gain, packed_out):
    count, slots, _ = parts.shape
    half_width = packed_out.shape[2] // 2
    room = heads // 2
    stats = parts[:, :, half_width:].astype(jnp.float32).reshape(count * slots, STATS)

    def term(number):
        return pltpu.roll(stats, STATS - number * room, 1) if number else stats

    peaks = (term(0) + term(1) + term(2)).reshape(count // 2, 2, slots, STATS)
    totals = (term(3) + term(4)).reshape(count // 2, 2, slots, STATS)
    lanes = lax.broadcasted_iota(jnp.int32, peaks.shape, 3)
    peaks = jnp.where(lanes < room, peaks, 0.0)
    factors = jnp.exp(peaks - jnp.max(peaks, axis=0, keepdims=True))
    total = jnp.sum(factors * totals, axis=0)
    spread_rows = lax.broadcasted_iota(jnp.int32, (STATS, half_width), 0)
    spread_cols = lax.broadcasted_iota(jnp.int32, (STATS, half_width), 1)
    spread = ((spread_cols // DH) == spread_rows).astype(jnp.float32)

    def spread_out(value):
        return lax.dot_general(
            value, spread, NN, precision=lax.Precision.HIGHEST, preferred_element_type=jnp.float32
        )

    wide = spread_out(factors.reshape(count * slots, STATS)).reshape(
        count // 2, 2, slots, half_width
    )
    numer = parts[:, :, :half_width].astype(jnp.float32).reshape(wide.shape)
    numer = jnp.sum(wide * numer, axis=0)
    wide_total = spread_out(total.reshape(2 * slots, STATS)).reshape(2, slots, half_width)
    ratio = numer / wide_total
    raw = jnp.concatenate([ratio[0], ratio[1]], axis=1)
    centred = raw - jnp.mean(raw, axis=1, keepdims=True)
    variance = jnp.mean(centred * centred, axis=1, keepdims=True)
    packed = (centred * lax.rsqrt(variance + 1e-06) * gain[...]).astype(jnp.bfloat16)
    packed_out[...] = jnp.broadcast_to(packed[None], packed_out.shape)


def tail_kernel(heads, packed_a, packed_b, query_fwd, query_rev, pairing, seat, *refs):
    own, near, near_swapped, far, far_swapped, out, queries, weight, attended = refs
    width = queries.shape[1]
    length = out.shape[0]
    x, core = seat[3], seat[2]
    block = width // X
    half = weight.shape[0] // 2

    def columns(number):
        return pl.ds(pl.multiple_of(lax.rem(number + X, X) * block, block), block)

    weight[:, columns(x)] = own[...]
    weight[:, columns(x + 2 * core - 1)] = near[...]
    weight[:, columns(x + 1 - 2 * core)] = near_swapped[...]
    weight[pl.ds(pl.multiple_of(core * half, half), half), columns(x + 2)] = far[...]
    weight[pl.ds(pl.multiple_of((1 - core) * half, half), half), columns(x + 2)] = far_swapped[...]
    queries[:length] = query_fwd[...]
    queries[length:] = query_rev[...]
    packed = jnp.concatenate([packed_a[...], packed_b[...]], axis=0)
    keys = dot(weight[:width], packed, NT).astype(jnp.bfloat16)
    values = dot(packed, weight[width : 2 * width], NT).astype(jnp.bfloat16)
    lanes = lax.broadcasted_iota(jnp.int32, (2 * length, 2 * DH), 1)
    slot_lanes = lax.broadcasted_iota(jnp.int32, (values.shape[0], 2 * DH), 1)
    for pair in range(heads // 2):
        cols = slice(pair * 2 * DH, (pair + 1) * 2 * DH)
        query_pair = queries[:, cols] * SCALE
        results = []
        for number in range(2):
            scores = dot(jnp.where(lanes // DH == number, query_pair, 0), keys[cols], NN)
            expo = jnp.exp(scores - jnp.max(scores, axis=1, keepdims=True)).astype(jnp.bfloat16)
            with_ones = jnp.where(slot_lanes // DH == number, values[:, cols], 1)
            results.append(dot(expo, with_ones, NN))
        numer = jnp.where(lanes < DH, *results)
        total = pltpu.roll(jnp.where(lanes < DH, *results[::-1]), DH, 1)
        attended[:, cols] = (numer / total).astype(jnp.bfloat16)
    order = lax.broadcasted_iota(jnp.int32, (length, length), 0)
    order = order + lax.broadcasted_iota(jnp.int32, (length, length), 1) == length - 1
    flipped = dot(order.astype(jnp.bfloat16), attended[length:], NN).astype(jnp.bfloat16)
    attended[length:] = flipped
    mixed = dot(attended[...], weight[2 * width :], NT)
    reverse = mixed[length:]
    upper = reverse.astype(jnp.bfloat16)
    lower = (reverse - upper.astype(jnp.float32)).astype(jnp.bfloat16)
    paired = dot(jnp.concatenate([upper, lower], axis=0), pairing[...], NN)
    paired = paired[:length] + paired[length:]
    out[...] = (mixed[:length] + paired).astype(jnp.bfloat16)


def params(mib):
    return pltpu.CompilerParams(vmem_limit_bytes=mib * MIB)


VMEM = pl.BlockSpec(memory_space=pltpu.VMEM)
HBM = pl.BlockSpec(memory_space=pltpu.HBM)
SMEM = pl.BlockSpec(memory_space=pltpu.SMEM)


def shards(
    tokens,
    fwd_states,
    rev_states,
    conv_weight,
    embedding,
    in_weight,
    pack_query,
    pack_gain,
    tail_weight,
    channel_perm,
):
    local_len = tokens.shape[0]
    width = fwd_states.shape[1]
    slots = pack_query.shape[0]
    heads = width // DH
    count = lax.axis_size("seq")
    own_slots = slots // count
    place = lax.axis_index("seq")
    x = lax.axis_index("batch") // 2
    core = place % 2
    seat = jnp.stack([place // (2 * Z), place // 2 % Z, core, x]).astype(jnp.int32)

    block = width // X
    tail_block = lax.dynamic_slice_in_dim(tail_weight.T, x * block, block, 1)
    shard = jnp.concatenate([in_weight.T, tail_block], axis=1)
    across = send(shard, Y_OPPOSITE)
    rims, opposite = strand_edges(tokens, fwd_states, rev_states)
    across, rims = lax.optimization_barrier((across, rims))
    held = [
        ((number,), jnp.stack([mine, send(mine, CORE_SWAP)]))
        for number, mine in enumerate((shard, across))
    ]
    pieces = [((halves, 0, False, False), piece) for halves, piece in held]
    pairing = (
        lax.broadcasted_iota(jnp.int32, (width, width), 0) == channel_perm[None, :]
    ).astype(jnp.bfloat16)
    x_own = strand_inputs(
        tokens, fwd_states, rev_states, rims, opposite, conv_weight, embedding
    )
    x_own, pairing = lax.optimization_barrier((x_own, pairing))
    x_other = send(x_own, CORE_SWAP)
    for step in range(1, Z // 2 + 1):
        held, brought = ring_step(held, step, core)
        pieces += brought
    places, pieces = zip(*pieces)

    fetched = pltpu.with_memory_space_constraint(pieces[LATE], pltpu.HBM)
    pieces = [*pieces[:LATE], fetched, *pieces[LATE + 1 :]]
    part, query_fwd, query_rev, own = pl.pallas_call(
        functools.partial(pack_kernel, places, heads),
        out_shape=(
            jax.ShapeDtypeStruct((slots, width // 2 + STATS), jnp.bfloat16),
            jax.ShapeDtypeStruct((local_len, width), jnp.bfloat16),
            jax.ShapeDtypeStruct((local_len, width), jnp.bfloat16),
            jax.ShapeDtypeStruct((3 * width, block), jnp.bfloat16),
        ),
        in_specs=[VMEM, VMEM, HBM, SMEM, VMEM, HBM] + [VMEM] * (len(pieces) - 2),
        out_specs=(VMEM,) * 4,
        scratch_shapes=[
            pltpu.VMEM((3 * width, width), jnp.bfloat16),
            pltpu.VMEM((4 * local_len, width), jnp.bfloat16),
            pltpu.VMEM(pieces[LATE].shape, jnp.bfloat16),
            pltpu.VMEM((slots, width), jnp.bfloat16),
            pltpu.SemaphoreType.DMA((2,)),
        ],
        compiler_params=params(20),
        name="pack",
    )(
        x_own,
        x_other,
        pltpu.with_memory_space_constraint(pack_query, pltpu.HBM),
        seat,
        *pieces,
    )

    near = send(own, X_RING)
    mirror = [(i, count - 1 - i) for i in range(count)]
    query_rev = lax.ppermute(query_rev, "seq", mirror)
    parts = lax.cond(
        place >= 0,
        lambda rows: lax.all_to_all(rows, "seq", 0, 0),
        lambda rows: rows,
        part.reshape(count, own_slots, -1),
    )
    parts, near, query_rev = lax.optimization_barrier((parts, near, query_rev))
    near_swapped = send(near, CORE_SWAP)
    half = 3 * width // 2
    far = send(lax.dynamic_slice_in_dim(near, core * half, half, 0), X_RING)
    copies = pl.pallas_call(
        functools.partial(merge_kernel, heads),
        out_shape=jax.ShapeDtypeStruct((count // 2, own_slots, width), jnp.bfloat16),
        in_specs=[VMEM, VMEM],
        out_specs=VMEM,
        compiler_params=params(12),
        name="merge",
    )(parts, pack_gain[None, :])

    same_core = [list(range(core, count, 2)) for core in range(2)]
    packed_a = lax.all_to_all(copies, "seq", 0, 0, axis_index_groups=same_core)
    packed_a = packed_a.reshape(slots // 2, width)
    packed_a, far, near_swapped = lax.optimization_barrier((packed_a, far, near_swapped))
    packed_b = send(packed_a, CORE_SWAP)
    far_swapped = send(far, CORE_SWAP)

    return pl.pallas_call(
        functools.partial(tail_kernel, heads),
        out_shape=jax.ShapeDtypeStruct((local_len, width), jnp.bfloat16),
        in_specs=[VMEM] * 5 + [SMEM] + [VMEM] * 5,
        out_specs=VMEM,
        scratch_shapes=[
            pltpu.VMEM((2 * local_len, width), jnp.bfloat16),
            pltpu.VMEM((3 * width, width), jnp.bfloat16),
            pltpu.VMEM((2 * local_len, width), jnp.bfloat16),
        ],
        compiler_params=params(20),
        name="tail",
    )(
        packed_a,
        packed_b,
        query_fwd,
        query_rev,
        pairing,
        seat,
        own,
        near,
        near_swapped,
        far,
        far_swapped,
    )


def solution(mesh):
    in_specs = (
        P(("batch", "seq")),
        P(("batch", "seq"), None),
        P(("batch", "seq"), None),
        P(),
        P(),
        P(None, "seq"),
        P(),
        P(),
        P(None, "seq"),
        P(),
    )
    out_specs = P(("batch", "seq"), None)
    return jax.shard_map(shards, mesh=mesh, in_specs=in_specs, out_specs=out_specs, check_vma=False)
```
